128 devices in a mesh: gx: 16 (over x, z_lo, core), gy: 8 (over y, z_hi).
Axes of the slice: x: 4, y: 4, z: 4 (z_hi: 2, z_lo: 2; z = z_hi * 2 + z_lo), core: 2. Of those that a mesh axis runs over, the one named last changes fastest.
Arguments:
- sources: float32 [262144, 128], P(('gx', 'gy')), may hold values from -6 to 6
- owner: int32 [262144, 1], P(('gx', 'gy')), may hold values from 0 to 127; in each aligned block of 2048 rows (0 to 2047, 2048 to 4095, ...) at most 32 rows name the same one
- box: int32 [262144], P(('gx', 'gy')), may hold values from 0 to 1023
- leaf_op: float32 [2, 64, 64], replicated, may hold values from -0.5 to 0.5
- level_ops: float32 [7, 2, 2, 2, 64, 64], replicated, may hold values from -0.375 to 0.375
- twiddle: float32 [7, 131072], P(None, ('gx', 'gy')), may hold values from -3.140625 to 3.140625
Outputs:
- weights: float32 [131072, 128], P(('gx', 'gy'))
The draws below stay inside these ranges and needn't reach their ends.
Inputs may be any that keep to these rules, and one draw needn't show every extreme that they name: Among the 2048 source blocks of one device, at most 32 name the same owner; in every draw some device has exactly 32 for one owner.
All inputs are finite; a program needn't handle non-finite values.
Results may differ from the reference program's by a relative error of at most 0.0003.
Values sent between devices are 32-bit elements; how exact they have to be, the bound alone decides.
No kernel may reach another device: no remote copies, remote signals or barrier semaphores. Data moves between devices by JAX's collectives and lax.ppermute only.
A program may use at most 64 MiB of HBM per device.

```python
import math
import jax
import jax.numpy as jnp
import numpy as np
from jax import lax

R = 64
K_BOX = 1024
SRC_DEV = 2048
CAP = 32
LEVELS = 7
BOXES = 131072
SOURCES = 262144
N_GX = 16
N_GY = 8
DEVICES = 128


def touch_ends(entries, key, least, top_value):
    longest = entries.shape.index(max(entries.shape))
    spots = []
    for shift in (0, 1):
        where = [jax.random.randint(jax.random.fold_in(key, axis), (), 0, length) for axis, length in enumerate(entries.shape)]
        where[longest] = (where[longest] + shift) % entries.shape[longest]
        spots.append(tuple(where))
    return entries.at[spots[0]].set(least).at[spots[1]].set(top_value)


def levels(own_key, extent, split, smallest, high):
    def one(position, blocks):
        draws = jax.random.uniform(jax.random.fold_in(jax.random.fold_in(own_key, 6), position), (blocks,), jnp.float32, smallest / len(split), high / len(split))
        return jnp.repeat(jnp.exp(draws), extent[position] // blocks).reshape((-1,) + (1,) * (len(extent) - position - 1))

    gain = one(*split[0])
    for cut in split[1:]:
        gain = gain * one(*cut)
    return gain


def deal_out(stream_key, own, number, rows, amount, top, most, lean):
    ranking = jax.random.permutation(stream_key, amount)
    crowded, ordinary = shares(amount, rows * top, most, lean, True), shares(amount, rows * top, most, lean, False)
    places = jnp.arange(amount)

    def named(lengths, rotation):
        used = int((lengths > 0).sum())
        fixed = max(1, used // 4)
        passed = fixed + (places - fixed + rotation * (used - fixed)) % max(1, amount - fixed)
        return jnp.zeros((amount,), jnp.int32).at[ranking[jnp.where(places < fixed, places, passed)]].set(jnp.asarray(lengths, jnp.int32))

    lengths = jnp.where(number % 4 == 0, named(crowded, number // 4), named(ordinary, number - number // 4 - 1))
    mixed = jax.random.permutation(jax.random.fold_in(own, 3), amount)
    donor, taker = mixed[0:amount // 2 * 2:2], mixed[1:amount // 2 * 2:2]
    room = jnp.minimum(lengths[donor] - 1, most - lengths[taker]) // 2
    room = jnp.where((donor == ranking[0]) | (taker == ranking[0]) | (lengths[taker] == 0), 0, jnp.maximum(room, 0))
    passed = jax.random.randint(jax.random.fold_in(own, 4), (amount // 2,), 0, 1 << 20) % (room + 1)
    lengths = lengths.at[donor].add(-passed).at[taker].add(passed)
    members = jnp.searchsorted(jnp.cumsum(lengths), jnp.arange(rows * top), side="right").astype(jnp.int32)
    listing = members.reshape(top, rows).T
    listing = listing[jax.random.permutation(jax.random.fold_in(own, 1), rows)]
    rotation = jax.random.randint(jax.random.fold_in(own, 2), (rows, 1), 0, top)
    return jnp.take_along_axis(listing, (jnp.arange(top)[None, :] + rotation) % top, axis=1)


def shares(number_of, total, most, skew, full):
    portions = [(1 << 20) // math.isqrt(grade ** skew) + 1 for grade in range(1, number_of + 1)]
    largest = most if full else min(most, max(-(-total // number_of), total * portions[0] // sum(portions)))
    least = 1 if total - largest >= number_of - 1 else 0
    given, surplus = [largest] + [least] * (number_of - 1), total - largest - least * (number_of - 1)
    while surplus > 0:
        free = [i for i in range(1, number_of) if given[i] < largest] or [i for i in range(1, number_of) if given[i] < most]
        mass, left = sum([portions[i] for i in free]), surplus
        for i in free:
            extra = min(most - given[i], max(1, left * portions[i] // mass), surplus)
            given[i] = given[i] + extra
            surplus = surplus - extra
    return np.array(given)


def normal_values(own_key, shape, scale, reach, shards=(), dtype=jnp.bfloat16):
    array = scale * jax.random.normal(own_key, shape, jnp.float32)
    if shards:
        array = array * levels(own_key, shape, shards, -0.22, 0.18)
    return jnp.clip(array, -reach, reach).astype(dtype)


def setup_inputs(seed: int = 0) -> dict:
    arg_keys = jax.random.split(jax.random.key(seed), 7)
    sources = normal_values(arg_keys[0], (SOURCES, 2 * R), 1.0, 6.0, ((0, 128),), jnp.float32)
    owner_keys = jax.random.split(jax.random.fold_in(arg_keys[1], 1), SOURCES // SRC_DEV)
    owner_turns = jax.random.permutation(jax.random.fold_in(arg_keys[1], 3), SOURCES // SRC_DEV)
    owner = jax.vmap(lambda own, number: deal_out(jax.random.fold_in(arg_keys[1], 2), own, number, SRC_DEV, DEVICES, 1, CAP, 1))(owner_keys, owner_turns).reshape((SOURCES, 1))
    box = touch_ends(jax.random.randint(arg_keys[2], (SOURCES,), 0, K_BOX), jax.random.fold_in(arg_keys[2], 1), 0, K_BOX - 1).astype(jnp.int32)
    leaf_op = normal_values(arg_keys[3], (2, R, R), (2 * R) ** -0.5, 0.5, (), jnp.float32)
    level_ops = normal_values(arg_keys[4], (LEVELS, 2, 2, 2, R, R), (4 * R) ** -0.5, 0.375, (), jnp.float32)
    twiddle = jnp.clip(jax.random.uniform(arg_keys[5], (LEVELS, BOXES), jnp.float32, -3.140625, 3.140625), -3.140625, 3.140625)
    return dict(sources=sources, owner=owner, box=box, leaf_op=leaf_op, level_ops=level_ops, twiddle=twiddle)


def complex_block(parts):
    real = parts[0]
    imag = parts[1]
    upper = jnp.concatenate([real, imag], axis=1)
    lower = jnp.concatenate([-imag, real], axis=1)
    return jnp.concatenate([upper, lower], axis=0)


def level_matrix(ops):
    from_low = jnp.concatenate([complex_block(ops[0, 0]), complex_block(ops[1, 0])], axis=1)
    from_high = jnp.concatenate([complex_block(ops[0, 1]), complex_block(ops[1, 1])], axis=1)
    return jnp.concatenate([from_low, from_high], axis=0)


def rotate(blocks, angle):
    half = blocks.shape[-1] // 2
    real = blocks[:, :half]
    imag = blocks[:, half:]
    cosine = jnp.cos(angle)[:, None]
    sine = jnp.sin(angle)[:, None]
    return jnp.concatenate([real * cosine - imag * sine, real * sine + imag * cosine], axis=1)


def reference(sources, owner, box, leaf_op, level_ops, twiddle):
    devices = N_GX * N_GY
    width = 2 * R
    target = (owner[:, 0] * K_BOX + box).astype(jnp.int32)
    gathered = jax.ops.segment_sum(sources, target, num_segments=BOXES)
    blocks = jnp.dot(gathered, complex_block(leaf_op), precision=lax.Precision.HIGHEST,
                     preferred_element_type=jnp.float32)
    blocks = blocks.reshape(devices, 2, K_BOX // 2, width)
    index = np.arange(devices)
    for level in range(LEVELS):
        parity = (index >> level) & 1
        low_dev = index & ~(1 << level)
        high_dev = low_dev | (1 << level)
        lower = blocks[low_dev, parity]
        upper = blocks[high_dev, parity]
        stacked = jnp.concatenate([lower, upper], axis=-1).reshape(-1, 2 * width)
        mixed = jnp.dot(stacked, level_matrix(level_ops[level]), precision=lax.Precision.HIGHEST,
                        preferred_element_type=jnp.float32)
        mixed = rotate(mixed.reshape(BOXES, width), twiddle[level])
        blocks = mixed.reshape(devices, 2, K_BOX // 2, width)
    return blocks.reshape(BOXES, width)
```

```python
import jax
import jax.numpy as jnp
from jax import lax
from jax.experimental import pallas as pl
from jax.experimental.pallas import tpu as pltpu
from jax.sharding import PartitionSpec as P

LANES = 128
VMEM_LIMIT = 48 * 1024 * 1024


def swapped(shard, axis, stride):
    return lax.ppermute(shard, axis, [(i, i ^ 1 << stride) for i in range(lax.axis_size(axis))])


def complex_block(parts):
    real = parts[0]
    imag = parts[1]
    upper = jnp.concatenate([real, imag], axis=1)
    lower = jnp.concatenate([-imag, real], axis=1)
    return jnp.concatenate([upper, lower], axis=0)


def level_matrix(ops):
    from_low = jnp.concatenate([complex_block(ops[0, 0]), complex_block(ops[1, 0])], axis=1)
    from_high = jnp.concatenate([complex_block(ops[0, 1]), complex_block(ops[1, 1])], axis=1)
    return jnp.concatenate([from_low, from_high], axis=0)


def rotate(blocks, angle):
    half = blocks.shape[-1] // 2
    real = blocks[:, :half]
    imag = blocks[:, half:]
    cosine = jnp.cos(angle)[:, None]
    sine = jnp.sin(angle)[:, None]
    return jnp.concatenate([real * cosine - imag * sine, real * sine + imag * cosine], axis=1)


def general(sources, owner, box, leaf_op, level_ops, twiddle):
    count_gx = lax.axis_size("gx")
    count_gy = lax.axis_size("gy")
    devices = count_gx * count_gy
    src_count = sources.shape[0]
    width = sources.shape[1]
    box_count = twiddle.shape[1]
    capacity = max(2, 2 * src_count // devices)
    destination = owner[:, 0]
    onehot = (destination[:, None] == jnp.arange(devices, dtype=jnp.int32)[None, :]).astype(
        jnp.int32
    )
    ranking = jnp.sum(jnp.cumsum(onehot, axis=0) * onehot, axis=1) - 1
    slot_index = destination * capacity + ranking
    packed = jnp.zeros((devices * capacity, width), jnp.float32).at[slot_index].set(sources)
    labels = jnp.full((devices * capacity,), box_count, jnp.int32).at[slot_index].set(box)
    arrived, arrived_labels = (
        lax.all_to_all(
            packed.reshape(devices, capacity, width),
            ("gx", "gy"),
            split_axis=0,
            concat_axis=0,
            tiled=True,
        ),
        lax.all_to_all(
            labels.reshape(devices, capacity), ("gx", "gy"), split_axis=0, concat_axis=0, tiled=True
        ),
    )
    gathered = jax.ops.segment_sum(
        arrived.reshape(-1, width), arrived_labels.reshape(-1), num_segments=box_count + 1
    )[:box_count]
    blocks = jnp.dot(
        gathered,
        complex_block(leaf_op),
        precision=lax.Precision.HIGHEST,
        preferred_element_type=jnp.float32,
    )
    bits_gy = count_gy.bit_length() - 1
    bits_gx = count_gx.bit_length() - 1
    for level in range(bits_gy + bits_gx):
        halves = blocks.reshape(2, box_count // 2, width)
        if level < bits_gy:
            parity = jnp.bitwise_and(jnp.right_shift(lax.axis_index("gy"), level), 1)
        else:
            parity = jnp.bitwise_and(jnp.right_shift(lax.axis_index("gx"), level - bits_gy), 1)
        upper_kept = parity == 1
        kept = jnp.where(upper_kept, halves[1], halves[0])
        outgoing = jnp.where(upper_kept, halves[0], halves[1])
        if level < bits_gy:
            incoming = swapped(outgoing, "gy", level)
        else:
            incoming = swapped(outgoing, "gx", level - bits_gy)
        lower = jnp.where(upper_kept, incoming, kept)
        upper = jnp.where(upper_kept, kept, incoming)
        stacked = jnp.concatenate([lower, upper], axis=1)
        mixed = jnp.dot(
            stacked,
            level_matrix(level_ops[level]),
            precision=lax.Precision.HIGHEST,
            preferred_element_type=jnp.float32,
        )
        blocks = rotate(mixed.reshape(box_count, width), twiddle[level])
    return blocks


SLOTS = 40
KEPT = SLOTS - 1
FLAG_LANE = 39
FIRST_LANE = 48
SECOND_LANE = 64
UNROLL = 32


def bit(value, place):
    return jnp.bitwise_and(jnp.right_shift(value, place), 1)


def bits_to(value, places):
    total = None
    for source, target in places:
        term = jnp.left_shift(bit(value, source), target)
        total = term if total is None else total + term
    return total


def iota(shape, axis):
    return lax.broadcasted_iota(jnp.int32, shape, axis)


def exact_dot(left, right, contract=(1, 0)):
    return lax.dot_general(
        left,
        right,
        (((contract[0],), (contract[1],)), ((), ())),
        precision=lax.Precision.HIGHEST,
        preferred_element_type=jnp.float32,
    )


def angles_for_all(twiddle_ref, level, lane):
    width = 16 << level
    devices = LANES
    dest = iota((devices, LANES), 0)
    cols = iota((devices, LANES), 1)
    first = bits_to(dest, [(level + 1 + b, 2 - b) for b in range(3)])
    last = range(level + 4, 7)
    group = bits_to(dest, [(b, 6 - b) for b in last])
    rows = jnp.zeros((devices, LANES), jnp.float32)
    for g in range(8):
        part = twiddle_ref[level : level + 1, g * LANES : (g + 1) * LANES]
        rows = jnp.where(first == g, part, rows)
    rows = jnp.where(jnp.right_shift(cols, 4 + level) == group, rows, 0.0)
    fold = jnp.where(cols == lane + jnp.bitwise_and(dest, width - 1), 1.0, 0.0)
    return exact_dot(rows, fold)


def pack_kernel(owner_ref, box_ref, src_ref, twiddle_ref, out_ref, slot_vmem, slot_smem, sem):
    chunks = owner_ref.shape[0]
    devices = LANES
    rows = iota((devices, LANES), 0)
    cols = iota((devices, LANES), 1)
    upto = jnp.where(rows <= cols, 1.0, 0.0).astype(jnp.bfloat16)
    high_half = rows < 64
    rank_of_row = jnp.bitwise_and(rows, 63)
    places = [(0, 9), (1, 8), (2, 7), (4, 6), (5, 5), (3, 4), (6, 3)]

    def rank_chunk(c, carried):
        count, labels = carried
        owner = owner_ref[pl.ds(c, 1), :]
        box = box_ref[pl.ds(c, 1), :]
        dest = bits_to(box, [(3 + b, 6 - b) for b in range(7)])
        target = bits_to(owner, places) + jnp.bitwise_and(box, 7) + 1
        hit = dest == rows
        onehot = jnp.where(hit, 1.0, 0.0).astype(jnp.bfloat16)
        upto_here = jnp.dot(onehot, upto, preferred_element_type=jnp.float32) + count
        rank = jnp.sum(jnp.where(hit, upto_here, 0.0), axis=0, keepdims=True) - 1.0
        rank = rank.astype(jnp.int32)
        slot_vmem[pl.ds(c, 1), :] = dest * SLOTS + jnp.minimum(rank, KEPT)
        part = jnp.where(high_half, jnp.right_shift(target, 5), jnp.bitwise_and(target, 31))
        part = jnp.where(rank == rank_of_row, part, 0).astype(jnp.float32).astype(jnp.bfloat16)
        labels = labels + lax.dot_general(
            onehot, part, (((1,), (1,)), ((), ())), preferred_element_type=jnp.float32
        )
        return upto_here[:, LANES - 1 : LANES], labels

    count = jnp.zeros((devices, 1), jnp.float32)
    labels = jnp.zeros((devices, LANES), jnp.float32)
    for c in range(chunks):
        count, labels = rank_chunk(c, (count, labels))
    copy = pltpu.make_async_copy(slot_vmem, slot_smem, sem)
    copy.start()

    def clear(n, carry):
        out_ref[pl.ds(pl.multiple_of(n * 64, 64), 64), :] = jnp.zeros((64, LANES), jnp.float32)
        return carry

    lax.fori_loop(0, out_ref.shape[0] // 64, clear, 0)
    most = jnp.max(count, axis=0, keepdims=True)
    over = jnp.where(most > float(KEPT), 1.0, 0.0)
    label_rows = labels * 32.0 + pltpu.roll(labels, 64, 1)
    label_rows = jnp.where(cols < KEPT, label_rows, jnp.where(cols == FLAG_LANE, over, 0.0))
    label_rows += angles_for_all(twiddle_ref, 0, FIRST_LANE)
    label_rows += angles_for_all(twiddle_ref, 1, SECOND_LANE)
    copy.wait()
    per_row = LANES // UNROLL

    def move(n, carry):
        c = n // per_row
        first = lax.rem(n, per_row) * UNROLL
        base = pl.multiple_of(n * UNROLL, UNROLL)
        for k in range(UNROLL):
            out_ref[pl.ds(slot_smem[c, first + k], 1), :] = src_ref[pl.ds(base + k, 1), :]
        return carry

    lax.fori_loop(0, chunks * per_row, move, 0)
    out_ref[pl.ds(KEPT, devices, stride=SLOTS), :] = label_rows


def in_vmem(count):
    return [pl.BlockSpec(memory_space=pltpu.VMEM)] * count


def pack(owner, box, sources, twiddle):
    count, width = sources.shape
    chunks = count // LANES
    return pl.pallas_call(
        pack_kernel,
        out_shape=jax.ShapeDtypeStruct((LANES * SLOTS, width), jnp.float32),
        in_specs=in_vmem(4),
        out_specs=in_vmem(1)[0],
        scratch_shapes=[
            pltpu.VMEM((chunks, LANES), jnp.int32),
            pltpu.SMEM((chunks, LANES), jnp.int32),
            pltpu.SemaphoreType.DMA,
        ],
        compiler_params=pltpu.CompilerParams(vmem_limit_bytes=VMEM_LIMIT),
    )(owner.reshape(chunks, LANES), box.reshape(chunks, LANES), sources, twiddle)


LAYOUTS = (
    ("e0", "D1", "D2", "D4", "D5", "D3", "D6"),
    ("e0", "e1", "D2", "D4", "D5", "D3", "D6"),
    ("e0", "e1", "e2", "D4", "D5", "D3", "D6"),
    ("D4", "D5", "e3", "e0", "e1", "e2", "D6"),
    ("e4", "D5", "e3", "e0", "e1", "e2", "D6"),
    ("e4", "e5", "e3", "e0", "e1", "e2", "D6"),
    ("e4", "e5", "e6", "e0", "e1", "e2", "e3"),
)
MASKS = 0x1241124
EXCHANGES_TO = 0x743


def twiddle_place(level, position, device):
    names = {}
    for place, name in enumerate(LAYOUTS[level]):
        names[name] = bit(position, 9 - place)
    for b in range(3):
        names["q" + str(b)] = bit(position, b)
    owner = 0
    for b in range(7):
        here = names["D" + str(b)] if b > level else bit(device, b)
        owner = owner + jnp.left_shift(here, b)
    order = [bit(device, b) for b in range(level + 1, 7)]
    order = order + [names["q2"], names["q1"], names["q0"]]
    order = order + [names["e" + str(b)] for b in range(level + 1)]
    index = 0
    for value in order:
        index = index * 2 + value
    return owner, index


def rotations(held, row, column, level, cos_ref, sin_ref):
    pick = jnp.where(row == iota((held.shape[0], 8 * LANES), 0), 1.0, 0.0)
    spread = exact_dot(held, pick, (0, 0))
    mine = column == iota((LANES, 8 * LANES), 0)
    angle = jnp.sum(jnp.where(mine, spread, 0.0), axis=0, keepdims=True)
    angle = jnp.concatenate([angle[:, c * LANES : (c + 1) * LANES] for c in range(8)], axis=0)
    cos_ref[level * 8 : level * 8 + 8, :] = jnp.cos(angle)
    sin_ref[level * 8 : level * 8 + 8, :] = jnp.sin(angle)


def split(value):
    high = value.astype(jnp.bfloat16)
    low = (value - high.astype(jnp.float32)).astype(jnp.bfloat16)
    return high, low


def prepare_kernel(
    dev_ref, far_ref, twiddle_ref, leaf_ref, ops_ref,
    cos_ref, sin_ref, leaf_h, leaf_l, mats_h, mats_l,
):
    device = dev_ref[0]
    position = iota((1, 8 * LANES), 1)
    cos_ref[0:16, :] = jnp.zeros((16, LANES), jnp.float32)
    sin_ref[0:16, :] = jnp.zeros((16, LANES), jnp.float32)
    for level in range(2, 7):
        owner, index = twiddle_place(level, position, device)
        column = jnp.bitwise_and(index, LANES - 1)
        if level < 6:
            row = jnp.bitwise_xor(jnp.right_shift(owner, 3), jnp.right_shift(device, 3))
            kept = max(1, 2 ** (level - 3))
            fixed = 0
            for b in range(level + 1, min(7, level + 4)):
                fixed = fixed * 2 + bit(device, b)
            parts = []
            for k in range(kept):
                lane = pl.multiple_of((fixed * kept + k) * LANES, LANES)
                parts.append(far_ref[:, pl.ds(lane, LANES)])
            held = jnp.concatenate(parts, axis=0)
            row = row * 4 + level - 2
            row = row + far_ref.shape[0] * jnp.bitwise_and(jnp.right_shift(index, 7), kept - 1)
        else:
            held = jnp.concatenate(
                [twiddle_ref[6:7, c * LANES : (c + 1) * LANES] for c in range(8)], axis=0
            )
            row = jnp.right_shift(index, 7)
        rotations(held, row, column, level, cos_ref, sin_ref)

    def block(real, imag):
        top = jnp.concatenate([real, imag], axis=1)
        bottom = jnp.concatenate([-imag, real], axis=1)
        return jnp.concatenate([top, bottom], axis=0).T

    leaf = block(leaf_ref[0], leaf_ref[1])
    leaf_h[...], leaf_l[...] = split(leaf)

    def build(n, carry):
        level, e, c = n // 4, lax.rem(n, 4) // 2, lax.rem(n, 2)
        high, low = split(block(ops_ref[level, e, c, 0], ops_ref[level, e, c, 1]))
        out = pl.ds(pl.multiple_of(e * LANES, LANES), LANES)
        across = pl.ds(pl.multiple_of(c * LANES, LANES), LANES)
        mats_h[level, out, across] = high
        mats_l[level, out, across] = low
        return carry

    lax.fori_loop(0, 4 * ops_ref.shape[0], build, 0, unroll=2)


def prepare(twiddle, leaf_op, level_ops):
    levels, count = twiddle.shape
    width = 2 * leaf_op.shape[1]
    device = lax.axis_index("gx") * lax.axis_size("gy") + lax.axis_index("gy")
    far = twiddle[2:6]
    for b in range(lax.axis_size("gx").bit_length() - 1):
        far = jnp.concatenate([far, swapped(far, "gx", b)], axis=0)
    return pl.pallas_call(
        prepare_kernel,
        out_shape=[
            jax.ShapeDtypeStruct((levels * count // LANES, LANES), jnp.float32),
            jax.ShapeDtypeStruct((levels * count // LANES, LANES), jnp.float32),
            jax.ShapeDtypeStruct((width, width), jnp.bfloat16),
            jax.ShapeDtypeStruct((width, width), jnp.bfloat16),
            jax.ShapeDtypeStruct((levels, 2 * width, 2 * width), jnp.bfloat16),
            jax.ShapeDtypeStruct((levels, 2 * width, 2 * width), jnp.bfloat16),
        ],
        in_specs=[pl.BlockSpec(memory_space=pltpu.SMEM)] + in_vmem(4),
        out_specs=in_vmem(6),
        compiler_params=pltpu.CompilerParams(vmem_limit_bytes=VMEM_LIMIT),
    )(device.reshape(1).astype(jnp.int32), far, twiddle, leaf_op, level_ops)


def product(high, low, value):
    value_high, value_low = split(value)
    total = jnp.dot(high, value_high, preferred_element_type=jnp.float32)
    total += jnp.dot(high, value_low, preferred_element_type=jnp.float32)
    total += jnp.dot(low, value_high, preferred_element_type=jnp.float32)
    return total


def nibble(table, n):
    return jnp.bitwise_and(jnp.right_shift(table, 4 * n), 15)


def finish_kernel(
    dev_ref, x_ref, cos_in, sin_in, leaf_h, leaf_l, mats_h, mats_l,
    out_ref, flag_ref, sums, names, state, cos_ref, sin_ref,
):
    devices = LANES
    device = dev_ref[0]
    half = LANES // 2
    labels = x_ref[pl.ds(KEPT, devices, stride=SLOTS), :]
    names[...] = labels.T - 1.0
    flag_ref[0] = jnp.max(names[FLAG_LANE : FLAG_LANE + 1, :] + 1.0).astype(jnp.int32)
    cos_ref[...] = cos_in[...]
    sin_ref[...] = sin_in[...]
    position = iota((1, 8 * LANES), 1)
    for level, lane in ((0, FIRST_LANE), (1, SECOND_LANE)):
        owner, index = twiddle_place(level, position, device)
        column = lane + jnp.bitwise_and(index, (16 << level) - 1)
        rotations(labels, owner, column, level, cos_ref, sin_ref)
    targets = iota((8 * LANES, 2 * LANES), 0).astype(jnp.float32)
    sums[...] = jnp.zeros_like(sums)

    def gather(pair, carry):
        rows = [x_ref[pl.ds(2 * pair + k, devices, stride=SLOTS), :] for k in range(2)]
        name = [names[pl.ds(2 * pair + k, 1), :] for k in range(2)]
        value = jnp.concatenate(rows, axis=0)
        pick = jnp.where(targets == jnp.concatenate(name, axis=1), 1.0, 0.0).astype(jnp.bfloat16)
        both = jnp.concatenate(split(value), axis=1)
        sums[...] += jnp.dot(pick, both, preferred_element_type=jnp.float32)
        return carry

    lax.fori_loop(0, SLOTS // 2, gather, 0)

    def leaf(c, carry):
        block = sums[pl.ds(pl.multiple_of(c * LANES, LANES), LANES), :]
        state[c] = product(leaf_h[...], leaf_l[...], (block[:, :LANES] + block[:, LANES:]).T)
        return carry

    lax.fori_loop(0, 8, leaf, 0)

    def pairs(mask):
        lows = [2 * n - jnp.bitwise_and(n, mask - 1) for n in range(4)]
        return [(low, low + mask) for low in lows]

    def level(number, carry):
        mask = nibble(MASKS, number)
        stacked = jnp.concatenate(
            [
                jnp.concatenate([state[pair[c]] for pair in pairs(mask)], axis=1)
                for c in range(2)
            ],
            axis=0,
        )
        mixed = product(mats_h[number], mats_l[number], stacked)
        for n, pair in enumerate(pairs(mask)):
            for e in range(2):
                block = mixed[e * LANES : (e + 1) * LANES, n * LANES : (n + 1) * LANES]
                real, imag = block[:half], block[half:]
                cosine = cos_ref[pl.ds(number * 8 + pair[e], 1), :]
                sine = sin_ref[pl.ds(number * 8 + pair[e], 1), :]
                state[pair[e], :half, :] = real * cosine - imag * sine
                state[pair[e], half:, :] = real * sine + imag * cosine
        return carry

    def exchange(number, carry):
        mask = nibble(MASKS, number)
        weight = jnp.right_shift(half, number)
        lane_set = jnp.bitwise_and(iota((LANES, LANES), 1), weight) != 0
        for low, high in pairs(mask):
            lower, upper = state[low], state[high]
            state[low] = jnp.where(lane_set, pltpu.roll(upper, weight, 1), lower)
            state[high] = jnp.where(lane_set, upper, pltpu.roll(lower, LANES - weight, 1))
        return carry

    def phase(number, done):
        lax.fori_loop(3 * number, jnp.minimum(3 * number + 3, 7), level, 0)
        then = nibble(EXCHANGES_TO, number)
        lax.fori_loop(done, then, exchange, 0)
        return then

    lax.fori_loop(0, 3, phase, 0)

    def write(c, carry):
        out_ref[pl.ds(pl.multiple_of(c * LANES, LANES), LANES), :] = state[c].T
        return carry

    lax.fori_loop(0, 8, write, 0)


def finish(arrived, prepared, box_count):
    width = arrived.shape[1]
    device = lax.axis_index("gx") * lax.axis_size("gy") + lax.axis_index("gy")
    table = pltpu.VMEM(prepared[0].shape, jnp.float32)
    return pl.pallas_call(
        finish_kernel,
        out_shape=[
            jax.ShapeDtypeStruct((box_count, width), jnp.float32),
            jax.ShapeDtypeStruct((1,), jnp.int32),
        ],
        in_specs=[pl.BlockSpec(memory_space=pltpu.SMEM)] + in_vmem(7),
        out_specs=[
            pl.BlockSpec(memory_space=pltpu.VMEM),
            pl.BlockSpec(memory_space=pltpu.SMEM),
        ],
        scratch_shapes=[
            pltpu.VMEM((box_count, 2 * width), jnp.float32),
            pltpu.VMEM((LANES, LANES), jnp.float32),
            pltpu.VMEM((8, width, LANES), jnp.float32),
            table,
            table,
        ],
        compiler_params=pltpu.CompilerParams(vmem_limit_bytes=VMEM_LIMIT),
    )(device.reshape(1).astype(jnp.int32), arrived, *prepared)


def local(sources, owner, box, leaf_op, level_ops, twiddle):
    width = sources.shape[1]
    box_count = twiddle.shape[1]
    packed = pack(owner, box, sources, twiddle)
    arrived = lax.all_to_all(
        packed.reshape(-1, SLOTS, width), ("gx", "gy"), split_axis=0, concat_axis=0, tiled=True
    ).reshape(-1, width)
    prepared = prepare(twiddle, leaf_op, level_ops)
    blocks, flag = finish(arrived, prepared, box_count)
    return lax.cond(
        flag[0] > 0,
        lambda: general(sources, owner, box, leaf_op, level_ops, twiddle),
        lambda: blocks,
    )


def solution(mesh):
    in_specs = (
        P(("gx", "gy"), None),
        P(("gx", "gy"), None),
        P(("gx", "gy")),
        P(),
        P(),
        P(None, ("gx", "gy")),
    )
    out_specs = P(("gx", "gy"), None)
    return jax.shard_map(local, mesh=mesh, in_specs=in_specs, out_specs=out_specs, check_vma=False)
```

```python
import jax
import jax.numpy as jnp
from jax import lax
from jax.experimental import pallas as pl
from jax.experimental.pallas import tpu as pltpu
from jax.sharding import PartitionSpec as P

LANES = 128
VMEM_LIMIT = 48 * 1024 * 1024


def swapped(shard, axis, shift):
    return lax.ppermute(shard, axis, [(i, i ^ shift) for i in range(lax.axis_size(axis))])


SLOTS = 40
KEPT = SLOTS - 1
FLAG_LANE = 39
FIRST_LANE = 48
SECOND_LANE = 64
SURE = 16
STEP = 4


def bit(value, place):
    return jnp.bitwise_and(jnp.right_shift(value, place), 1)


def bits_to(value, places):
    total = None
    for source, target in places:
        term = jnp.left_shift(bit(value, source), target)
        total = term if total is None else total + term
    return total


def iota(shape, axis):
    return lax.broadcasted_iota(jnp.int32, shape, axis)


def exact_dot(left, right, contract=(1, 0)):
    return lax.dot_general(
        left,
        right,
        (((contract[0],), (contract[1],)), ((), ())),
        precision=lax.Precision.HIGHEST,
        preferred_element_type=jnp.float32,
    )


def angles_for_all(twiddle_ref, level, lane):
    width = 16 << level
    devices = LANES
    dest = iota((devices, LANES), 0)
    cols = iota((devices, LANES), 1)
    first = bits_to(dest, [(level + 1 + b, 2 - b) for b in range(3)])
    last = range(level + 4, 7)
    group = bits_to(dest, [(b, 6 - b) for b in last])
    rows = jnp.zeros((devices, LANES), jnp.float32)
    for g in range(8):
        part = twiddle_ref[level : level + 1, g * LANES : (g + 1) * LANES]
        rows = jnp.where(first == g, part, rows)
    rows = jnp.where(jnp.right_shift(cols, 4 + level) == group, rows, 0.0)
    fold = jnp.where(cols == lane + jnp.bitwise_and(dest, width - 1), 1.0, 0.0)
    return exact_dot(rows, fold)


def rank_kernel(
    round_ref, owner_hbm, box_hbm, twiddle_hbm, slot_ref, label_ref, owner_ref, box_ref, twiddle_ref, sems
):
    pairs = ((owner_hbm, owner_ref), (box_hbm, box_ref), (twiddle_hbm, twiddle_ref))
    copies = [pltpu.make_async_copy(a, b, sems.at[n]) for n, (a, b) in enumerate(pairs)]
    for copy in copies:
        copy.start()
    for copy in copies:
        copy.wait()
    chunks = owner_ref.shape[0]
    devices = LANES
    passed = round_ref[0] * KEPT
    rows = iota((devices, LANES), 0)
    cols = iota((devices, LANES), 1)
    upto = jnp.where(rows <= cols, 1.0, 0.0).astype(jnp.bfloat16)
    high_half = rows < 64
    rank_of_row = jnp.bitwise_and(rows, 63)
    owner = owner_ref[...]
    box = box_ref[...]
    dest = bits_to(box, [(3 + b, 6 - b) for b in range(7)])
    places = [(0, 9), (1, 8), (2, 7), (4, 6), (5, 5), (3, 4), (6, 3)]
    target = bits_to(owner, places) + jnp.bitwise_and(box, 7) + 1
    target_high = jnp.right_shift(target, 5)
    target_low = jnp.bitwise_and(target, 31)
    count = jnp.zeros((devices, 1), jnp.float32)
    labels = jnp.zeros((devices, LANES), jnp.float32)
    for c in range(chunks):
        dest_c = dest[c : c + 1, :]
        hit = dest_c == rows
        onehot = jnp.where(hit, 1.0, 0.0).astype(jnp.bfloat16)
        upto_here = jnp.dot(onehot, upto, preferred_element_type=jnp.float32) + count
        rank = jnp.sum(jnp.where(hit, upto_here, 0.0), axis=0, keepdims=True) - 1.0
        count = upto_here[:, LANES - 1 : LANES]
        rank = rank.astype(jnp.int32) - passed
        now = jnp.logical_and(rank >= 0, rank < KEPT)
        slot_ref[c : c + 1, :] = dest_c * SLOTS + jnp.where(now, rank, KEPT)
        part = jnp.where(high_half, target_high[c : c + 1, :], target_low[c : c + 1, :])
        part = jnp.where(rank == rank_of_row, part, 0).astype(jnp.float32).astype(jnp.bfloat16)
        labels = labels + lax.dot_general(
            onehot, part, (((1,), (1,)), ((), ())), preferred_element_type=jnp.float32
        )
    most = jnp.max(count, axis=0, keepdims=True)
    left = jnp.where(most > (passed + KEPT).astype(jnp.float32), 1.0, 0.0)
    label_rows = labels * 32.0 + pltpu.roll(labels, 64, 1)
    label_rows = jnp.where(cols < KEPT, label_rows, jnp.where(cols == FLAG_LANE, left, 0.0))
    label_rows += angles_for_all(twiddle_ref, 0, FIRST_LANE)
    label_rows += angles_for_all(twiddle_ref, 1, SECOND_LANE)
    label_ref[...] = label_rows


def move_kernel(slot_hbm, label_ref, src_ref, after_hbm, out_ref, slot_smem, sem):
    del after_hbm
    devices = LANES
    chunks = slot_smem.shape[0]
    slots = pltpu.make_async_copy(slot_hbm, slot_smem, sem)
    slots.start()

    def clear(n, carry):
        out_ref[pl.ds(pl.multiple_of(n * 64, 64), 64), :] = jnp.zeros((64, LANES), jnp.float32)
        return carry

    lax.fori_loop(0, out_ref.shape[0] // 64, clear, 0)
    slots.wait()

    def move(c, carry):
        base = pl.multiple_of(c * LANES, LANES)
        for k in range(LANES):
            out_ref[pl.ds(slot_smem[c, k], 1), :] = src_ref[pl.ds(base + k, 1), :]
        return carry

    lax.fori_loop(0, chunks, move, 0)
    out_ref[pl.ds(KEPT, devices, stride=SLOTS), :] = label_ref[...]


def params():
    return pltpu.CompilerParams(vmem_limit_bytes=VMEM_LIMIT)


def in_vmem(count):
    return [pl.BlockSpec(memory_space=pltpu.VMEM)] * count


def anywhere(count):
    return [pl.BlockSpec(memory_space=pl.ANY)] * count


def in_smem():
    return [pl.BlockSpec(memory_space=pltpu.SMEM)]


def rank(number, owner, box, twiddle):
    chunks = owner.shape[0] // LANES
    block = pltpu.VMEM((chunks, LANES), jnp.int32)
    return pl.pallas_call(
        rank_kernel,
        out_shape=[
            jax.ShapeDtypeStruct((chunks, LANES), jnp.int32),
            jax.ShapeDtypeStruct((LANES, LANES), jnp.float32),
        ],
        in_specs=in_smem() + anywhere(3),
        out_specs=in_vmem(2),
        scratch_shapes=[
            block,
            block,
            pltpu.VMEM(twiddle.shape, jnp.float32),
            pltpu.SemaphoreType.DMA((3,)),
        ],
        compiler_params=params(),
    )(number.reshape(1), owner.reshape(chunks, LANES), box.reshape(chunks, LANES), twiddle)


def move(slots, labels, sources, after):
    return pl.pallas_call(
        move_kernel,
        out_shape=jax.ShapeDtypeStruct((LANES * SLOTS, sources.shape[1]), jnp.float32),
        in_specs=anywhere(1) + in_vmem(2) + anywhere(1),
        out_specs=in_vmem(1)[0],
        scratch_shapes=[
            pltpu.SMEM(slots.shape, jnp.int32),
            pltpu.SemaphoreType.DMA,
        ],
        compiler_params=params(),
    )(slots, labels, sources, after)


def deliver(packed):
    width = packed.shape[1]
    return lax.all_to_all(
        packed.reshape(-1, SLOTS, width), ("gx", "gy"), split_axis=0, concat_axis=0, tiled=True
    ).reshape(-1, width)


LAYOUTS = (
    ("e0", "D1", "D2", "D4", "D5", "D3", "D6"),
    ("e0", "e1", "D2", "D4", "D5", "D3", "D6"),
    ("e0", "e1", "e2", "D4", "D5", "D3", "D6"),
    ("D4", "D5", "e3", "e0", "e1", "e2", "D6"),
    ("e4", "D5", "e3", "e0", "e1", "e2", "D6"),
    ("e4", "e5", "e3", "e0", "e1", "e2", "D6"),
    ("e4", "e5", "e6", "e0", "e1", "e2", "e3"),
)
MASKS = 0x1241124
EXCHANGES_TO = 0x743


def twiddle_place(level, position, device):
    names = {}
    for place, name in enumerate(LAYOUTS[level]):
        names[name] = bit(position, 9 - place)
    for b in range(3):
        names["q" + str(b)] = bit(position, b)
    owner = 0
    for b in range(7):
        here = names["D" + str(b)] if b > level else bit(device, b)
        owner = owner + jnp.left_shift(here, b)
    order = [bit(device, b) for b in range(level + 1, 7)]
    order = order + [names["q2"], names["q1"], names["q0"]]
    order = order + [names["e" + str(b)] for b in range(level + 1)]
    index = 0
    for value in order:
        index = index * 2 + value
    return owner, index


def rotations(held, row, column, level, cos_ref, sin_ref):
    pick = jnp.where(row == iota((held.shape[0], 8 * LANES), 0), 1.0, 0.0)
    spread = exact_dot(held, pick, (0, 0))
    mine = column == iota((LANES, 8 * LANES), 0)
    angle = jnp.sum(jnp.where(mine, spread, 0.0), axis=0, keepdims=True)
    angle = jnp.concatenate([angle[:, c * LANES : (c + 1) * LANES] for c in range(8)], axis=0)
    cos_ref[level * 8 : level * 8 + 8, :] = jnp.cos(angle)
    sin_ref[level * 8 : level * 8 + 8, :] = jnp.sin(angle)


def split(value):
    high = value.astype(jnp.bfloat16)
    low = (value - high.astype(jnp.float32)).astype(jnp.bfloat16)
    return high, low


def prepare_kernel(
    dev_ref, far0, far1, far2, far3, twiddle_ref, leaf_ref, ops_ref,
    cos_ref, sin_ref, leaf_h, leaf_l, mats_h, mats_l,
):
    device = dev_ref[0]
    position = iota((1, 8 * LANES), 1)
    cos_ref[0:16, :] = jnp.zeros((16, LANES), jnp.float32)
    sin_ref[0:16, :] = jnp.zeros((16, LANES), jnp.float32)
    for level in range(2, 7):
        owner, index = twiddle_place(level, position, device)
        column = jnp.bitwise_and(index, LANES - 1)
        if level < 6:
            row = jnp.bitwise_xor(jnp.right_shift(owner, 3), jnp.right_shift(device, 3))
            kept = max(1, 2 ** (level - 3))
            fixed = 0
            for b in range(level + 1, min(7, level + 4)):
                fixed = fixed * 2 + bit(device, b)
            parts = []
            for k in range(kept):
                lane = pl.multiple_of((fixed * kept + k) * LANES, LANES)
                parts += [far[:, pl.ds(lane, LANES)] for far in (far0, far1, far2, far3)]
            held = jnp.concatenate(parts, axis=0)
            close = jnp.bitwise_and(row, 3)
            if level == 2:
                place = jnp.where(close == 0, 0, jnp.where(close == 3, 7, 3 + close))
            elif level == 3:
                place = 1 + jnp.where(close == 2, 5, 0)
            else:
                place = level - 2
            row = jnp.right_shift(row, 2) * far0.shape[0] + place
            row = row + 4 * far0.shape[0] * jnp.bitwise_and(jnp.right_shift(index, 7), kept - 1)
        else:
            held = jnp.concatenate(
                [twiddle_ref[6:7, c * LANES : (c + 1) * LANES] for c in range(8)], axis=0
            )
            row = jnp.right_shift(index, 7)
        rotations(held, row, column, level, cos_ref, sin_ref)

    def block(real, imag):
        top = jnp.concatenate([real, imag], axis=1)
        bottom = jnp.concatenate([-imag, real], axis=1)
        return jnp.concatenate([top, bottom], axis=0).T

    leaf = block(leaf_ref[0], leaf_ref[1])
    leaf_h[...], leaf_l[...] = split(leaf)

    def build(n, carry):
        level, e, c = n // 4, lax.rem(n, 4) // 2, lax.rem(n, 2)
        high, low = split(block(ops_ref[level, e, c, 0], ops_ref[level, e, c, 1]))
        out = pl.ds(pl.multiple_of(e * LANES, LANES), LANES)
        across = pl.ds(pl.multiple_of(c * LANES, LANES), LANES)
        mats_h[level, out, across] = high
        mats_l[level, out, across] = low
        return carry

    lax.fori_loop(0, 4 * ops_ref.shape[0], build, 0, unroll=2)


def prepare(twiddle, far, leaf_op, level_ops):
    levels, count = twiddle.shape
    width = 2 * leaf_op.shape[1]
    return pl.pallas_call(
        prepare_kernel,
        out_shape=[
            jax.ShapeDtypeStruct((levels * count // LANES, LANES), jnp.float32),
            jax.ShapeDtypeStruct((levels * count // LANES, LANES), jnp.float32),
            jax.ShapeDtypeStruct((width, width), jnp.bfloat16),
            jax.ShapeDtypeStruct((width, width), jnp.bfloat16),
            jax.ShapeDtypeStruct((levels, 2 * width, 2 * width), jnp.bfloat16),
            jax.ShapeDtypeStruct((levels, 2 * width, 2 * width), jnp.bfloat16),
        ],
        in_specs=in_smem() + in_vmem(7),
        out_specs=in_vmem(6),
        compiler_params=params(),
    )(own_number(), *far, twiddle, leaf_op, level_ops)


def own_number():
    device = lax.axis_index("gx") * lax.axis_size("gy") + lax.axis_index("gy")
    return device.reshape(1).astype(jnp.int32)


def product(high, low, value):
    value_high, value_low = split(value)
    total = jnp.dot(high, value_high, preferred_element_type=jnp.float32)
    total += jnp.dot(high, value_low, preferred_element_type=jnp.float32)
    total += jnp.dot(low, value_high, preferred_element_type=jnp.float32)
    return total


def angle_rows(labels, device, cos_ref, sin_ref):
    position = iota((1, 8 * LANES), 1)
    for level, lane in ((0, FIRST_LANE), (1, SECOND_LANE)):
        owner, index = twiddle_place(level, position, device)
        column = lane + jnp.bitwise_and(index, (16 << level) - 1)
        rotations(labels, owner, column, level, cos_ref, sin_ref)


def add_rows(x_ref, names, first, count):
    ranks = [first + k for k in range(count)]
    value = jnp.concatenate([x_ref[pl.ds(r, LANES, stride=SLOTS), :] for r in ranks], axis=0)
    name = jnp.concatenate([names[pl.ds(r, 1), :] for r in ranks], axis=1)
    targets = iota((8 * LANES, count * LANES), 0).astype(jnp.float32)
    pick = jnp.where(targets == name, 1.0, 0.0).astype(jnp.bfloat16)
    both = jnp.concatenate(split(value), axis=1)
    return jnp.dot(pick, both, preferred_element_type=jnp.float32)


def chunk_pairs(mask):
    lows = [2 * n - (n & (mask - 1)) for n in range(4)]
    return [(low, low + mask) for low in lows]


def nibble(table, n):
    return (table >> (4 * n)) & 15


def exchange(state, mask, weight):
    lane_set = jnp.bitwise_and(iota((LANES, LANES), 1), weight) != 0
    out = list(state)
    for low, high in chunk_pairs(mask):
        lower, upper = state[low], state[high]
        out[low] = jnp.where(lane_set, pltpu.roll(upper, weight, 1), lower)
        out[high] = jnp.where(lane_set, upper, pltpu.roll(lower, LANES - weight, 1))
    return out


def butterfly(state, mask, high, low, cos_ref, sin_ref, number):
    half = LANES // 2
    stacked = jnp.concatenate(
        [jnp.concatenate([state[pair[c]] for pair in chunk_pairs(mask)], axis=1) for c in range(2)],
        axis=0,
    )
    mixed = product(high, low, stacked)
    out = list(state)
    for n, pair in enumerate(chunk_pairs(mask)):
        for e in range(2):
            block = mixed[e * LANES : (e + 1) * LANES, n * LANES : (n + 1) * LANES]
            real, imag = block[:half], block[half:]
            place = number * 8 + pair[e]
            cosine = cos_ref[place : place + 1, :]
            sine = sin_ref[place : place + 1, :]
            out[pair[e]] = jnp.concatenate(
                [real * cosine - imag * sine, real * sine + imag * cosine], axis=0
            )
    return out


def finish_kernel(
    dev_ref, x_ref, cos_in, sin_in, leaf_h_in, leaf_l_in, mats_h_in, mats_l_in,
    out_ref, flag_ref,
    sums, names, cos_ref, sin_ref, cos_far, sin_far, leaf_h, leaf_l, mats_h, mats_l, sems,
):
    pairs = (
        (cos_in, cos_far), (sin_in, sin_far), (leaf_h_in, leaf_h), (leaf_l_in, leaf_l),
        (mats_h_in, mats_h), (mats_l_in, mats_l),
    )
    copies = [pltpu.make_async_copy(a, b, sems.at[n]) for n, (a, b) in enumerate(pairs)]
    for copy in copies:
        copy.start()
    labels = x_ref[pl.ds(KEPT, LANES, stride=SLOTS), :]
    names[...] = labels.T - 1.0
    flag_ref[0] = jnp.max(names[FLAG_LANE : FLAG_LANE + 1, :] + 1.0).astype(jnp.int32)
    column = iota((LANES, LANES), 1)
    filled = jnp.logical_and(labels > 0.0, column < KEPT)
    most = jnp.max(jnp.where(filled, column + 1, 0).astype(jnp.float32)).astype(jnp.int32)
    sums[...] = add_rows(x_ref, names, 0, SURE)
    angle_rows(labels, dev_ref[0], cos_ref, sin_ref)
    for first in range(SURE, SLOTS, STEP):

        @pl.when(most > first)
        def _():
            sums[...] += add_rows(x_ref, names, first, STEP)

    for copy in copies:
        copy.wait()
    cos_ref[16:, :] = cos_far[16:, :]
    sin_ref[16:, :] = sin_far[16:, :]
    state = []
    for c in range(8):
        block = sums[c * LANES : (c + 1) * LANES, :]
        state.append((block[:, :LANES] + block[:, LANES:]).T)
    leafed = product(leaf_h[...], leaf_l[...], jnp.concatenate(state, axis=1))
    state = [leafed[:, c * LANES : (c + 1) * LANES] for c in range(8)]
    done = 0
    for number in range(7):
        mask = nibble(MASKS, number)
        state = butterfly(state, mask, mats_h[number], mats_l[number], cos_ref, sin_ref, number)
        if number in (2, 5, 6):
            then = nibble(EXCHANGES_TO, number // 3)
            for n in range(done, then):
                state = exchange(state, nibble(MASKS, n), LANES // 2 >> n)
            done = then
    for c in range(8):
        out_ref[c * LANES : (c + 1) * LANES, :] = state[c].T


def finish(arrived, prepared, box_count):
    width = arrived.shape[1]
    table = pltpu.VMEM(prepared[0].shape, jnp.float32)
    return pl.pallas_call(
        finish_kernel,
        out_shape=[
            jax.ShapeDtypeStruct((box_count, width), jnp.float32),
            jax.ShapeDtypeStruct((1,), jnp.int32),
        ],
        in_specs=in_smem() + in_vmem(1) + anywhere(6),
        out_specs=in_vmem(1) + in_smem(),
        scratch_shapes=[
            pltpu.VMEM((box_count, 2 * width), jnp.float32),
            pltpu.VMEM((LANES, LANES), jnp.float32),
            table,
            table,
        ]
        + [pltpu.VMEM(array.shape, array.dtype) for array in prepared]
        + [pltpu.SemaphoreType.DMA((len(prepared),))],
        compiler_params=params(),
    )(own_number(), arrived, *prepared)


def collect_kernel(x_ref, before_ref, sums, label_ref, flag_ref, names):
    labels = x_ref[pl.ds(KEPT, LANES, stride=SLOTS), :]
    label_ref[...] = labels
    names[...] = labels.T - 1.0
    flag_ref[0] = jnp.max(names[FLAG_LANE : FLAG_LANE + 1, :] + 1.0).astype(jnp.int32)
    names[FLAG_LANE : FLAG_LANE + 1, :] = jnp.full((1, LANES), -1.0)
    sums[...] = before_ref[...]

    def body(pair, carry):
        sums[...] += add_rows(x_ref, names, 2 * pair, 2)
        return carry

    lax.fori_loop(0, SLOTS // 2, body, 0)


def collect(arrived, sums):
    return pl.pallas_call(
        collect_kernel,
        out_shape=[
            jax.ShapeDtypeStruct(sums.shape, jnp.float32),
            jax.ShapeDtypeStruct((LANES, LANES), jnp.float32),
            jax.ShapeDtypeStruct((1,), jnp.int32),
        ],
        in_specs=in_vmem(2),
        out_specs=in_vmem(2) + in_smem(),
        scratch_shapes=[pltpu.VMEM((LANES, LANES), jnp.float32)],
        compiler_params=params(),
    )(arrived, sums)


def levels_kernel(
    dev_ref, sums, labels_ref, cos_in, sin_in, leaf_h, leaf_l, mats_h, mats_l,
    out_ref, state, cos_ref, sin_ref,
):
    half = LANES // 2
    cos_ref[...] = cos_in[...]
    sin_ref[...] = sin_in[...]
    angle_rows(labels_ref[...], dev_ref[0], cos_ref, sin_ref)

    def leaf(c, carry):
        block = sums[pl.ds(pl.multiple_of(c * LANES, LANES), LANES), :]
        state[c] = product(leaf_h[...], leaf_l[...], (block[:, :LANES] + block[:, LANES:]).T)
        return carry

    lax.fori_loop(0, 8, leaf, 0)

    def level(number, carry):
        pairs = chunk_pairs(nibble(MASKS, number))
        stacked = jnp.concatenate(
            [jnp.concatenate([state[pair[c]] for pair in pairs], axis=1) for c in range(2)], axis=0
        )
        mixed = product(mats_h[number], mats_l[number], stacked)
        for n, pair in enumerate(pairs):
            for e in range(2):
                block = mixed[e * LANES : (e + 1) * LANES, n * LANES : (n + 1) * LANES]
                real, imag = block[:half], block[half:]
                cosine = cos_ref[pl.ds(number * 8 + pair[e], 1), :]
                sine = sin_ref[pl.ds(number * 8 + pair[e], 1), :]
                state[pair[e], :half, :] = real * cosine - imag * sine
                state[pair[e], half:, :] = real * sine + imag * cosine
        return carry

    def swap(number, carry):
        weight = half >> number
        lane_set = jnp.bitwise_and(iota((LANES, LANES), 1), weight) != 0
        for low, high in chunk_pairs(nibble(MASKS, number)):
            lower, upper = state[low], state[high]
            state[low] = jnp.where(lane_set, pltpu.roll(upper, weight, 1), lower)
            state[high] = jnp.where(lane_set, upper, pltpu.roll(lower, LANES - weight, 1))
        return carry

    def phase(number, done):
        lax.fori_loop(3 * number, jnp.minimum(3 * number + 3, 7), level, 0)
        then = nibble(EXCHANGES_TO, number)
        lax.fori_loop(done, then, swap, 0)
        return then

    lax.fori_loop(0, 3, phase, 0)

    def write(c, carry):
        out_ref[pl.ds(pl.multiple_of(c * LANES, LANES), LANES), :] = state[c].T
        return carry

    lax.fori_loop(0, 8, write, 0)


def transform(sums, labels, prepared):
    box_count, width = sums.shape[0], sums.shape[1] // 2
    table = pltpu.VMEM(prepared[0].shape, jnp.float32)
    return pl.pallas_call(
        levels_kernel,
        out_shape=jax.ShapeDtypeStruct((box_count, width), jnp.float32),
        in_specs=in_smem() + in_vmem(8),
        out_specs=in_vmem(1)[0],
        scratch_shapes=[pltpu.VMEM((8, width, LANES), jnp.float32), table, table],
        compiler_params=params(),
    )(own_number(), sums, labels, *prepared)


def in_rounds(sources, owner, box, twiddle, prepared):
    box_count, width = twiddle.shape[1], sources.shape[1]

    def body(carry):
        number, sums, _, _ = carry
        slots, labels = rank(number, owner, box, twiddle)
        arrived = deliver(move(slots, labels, sources, labels))
        return (number + 1, *collect(arrived, sums))

    start = (
        jnp.int32(0),
        jnp.zeros((box_count, 2 * width), jnp.float32),
        jnp.zeros((LANES, LANES), jnp.float32),
        jnp.ones((1,), jnp.int32),
    )
    _, sums, labels, _ = lax.while_loop(lambda carry: carry[3][0] > 0, body, start)
    return transform(sums, labels, prepared)


def local(sources, owner, box, leaf_op, level_ops, twiddle):
    box_count = twiddle.shape[1]
    near = [swapped(twiddle, "gx", i) for i in (1, 2, 3)]
    slots, labels = rank(jnp.int32(0), owner, box, twiddle)
    slots, labels, *near = lax.optimization_barrier((slots, labels, *near))
    near = jnp.concatenate([twiddle[2:6], near[0][2:3], near[1][2:4], near[2][2:3]], axis=0)
    packed = move(slots, labels, sources, near)
    far = [near] + [swapped(near, "gx", i) for i in (4, 8, 12)]
    packed, *far = lax.optimization_barrier((packed, *far))
    arrived = deliver(packed)
    prepared = prepare(twiddle, far, leaf_op, level_ops)
    blocks, flag = finish(arrived, prepared, box_count)
    return lax.cond(
        flag[0] > 0,
        lambda: in_rounds(sources, owner, box, twiddle, prepared),
        lambda: blocks,
    )


def solution(mesh):
    in_specs = (
        P(("gx", "gy"), None),
        P(("gx", "gy"), None),
        P(("gx", "gy")),
        P(),
        P(),
        P(None, ("gx", "gy")),
    )
    out_specs = P(("gx", "gy"), None)
    return jax.shard_map(local, mesh=mesh, in_specs=in_specs, out_specs=out_specs, check_vma=False)
```

```python
import jax
import jax.numpy as jnp
from jax import lax
from jax.experimental import pallas as pl
from jax.experimental.pallas import tpu as pltpu
from jax.sharding import PartitionSpec as P

LANES = 128
VMEM_LIMIT = 48 * 1024 * 1024


def swapped(shard, axis, shift):
    return lax.ppermute(shard, axis, [(i, i ^ shift) for i in range(lax.axis_size(axis))])


SLOTS = 40
KEPT = SLOTS - 2
LABEL_ROW = KEPT
FLAG_LANE = KEPT
ANGLE_ROW = KEPT + 1
ANGLE_LANES = (0, 32, 64)
THIRD_ROW = KEPT - 1
SURE = 16
STEP = 4


def bit(value, place):
    return jnp.bitwise_and(jnp.right_shift(value, place), 1)


def bits_to(value, places):
    total = None
    for source, target in places:
        term = jnp.left_shift(bit(value, source), target)
        total = term if total is None else total + term
    return total


def iota(shape, axis):
    return lax.broadcasted_iota(jnp.int32, shape, axis)


def exact_dot(left, right, contract=(1, 0)):
    return lax.dot_general(
        left,
        right,
        (((contract[0],), (contract[1],)), ((), ())),
        precision=lax.Precision.HIGHEST,
        preferred_element_type=jnp.float32,
    )


def angles_for_all(twiddle_ref, level, lane):
    width = 16 << level
    devices = LANES
    dest = iota((devices, LANES), 0)
    cols = iota((devices, LANES), 1)
    first = bits_to(dest, [(level + 1 + b, 2 - b) for b in range(3)])
    last = range(level + 4, 7)
    group = bits_to(dest, [(b, 6 - b) for b in last])
    rows = jnp.zeros((devices, LANES), jnp.float32)
    for g in range(8):
        part = twiddle_ref[level : level + 1, g * LANES : (g + 1) * LANES]
        rows = jnp.where(first == g, part, rows)
    rows = jnp.where(jnp.right_shift(cols, 4 + level) == group, rows, 0.0)
    fold = jnp.where(cols == lane + jnp.bitwise_and(dest, width - 1), 1.0, 0.0)
    return exact_dot(rows, fold)


def pack_kernel(
    round_ref, dev_ref, owner_hbm, box_hbm, twiddle_hbm, src_hbm, out_ref,
    owner_ref, box_ref, twiddle_ref, src_ref, slot_vmem, slot_smem, sems,
):
    pairs = (
        (owner_hbm, owner_ref), (box_hbm, box_ref), (twiddle_hbm, twiddle_ref), (src_hbm, src_ref),
        (slot_vmem, slot_smem),
    )
    copies = [pltpu.make_async_copy(a, b, sems.at[n]) for n, (a, b) in enumerate(pairs)]
    for copy in copies[:4]:
        copy.start()

    def clear(n, carry):
        out_ref[pl.ds(pl.multiple_of(n * 64, 64), 64), :] = jnp.zeros((64, LANES), jnp.float32)
        return carry

    lax.fori_loop(0, out_ref.shape[0] // 64, clear, 0)
    copies[0].wait()
    copies[1].wait()
    chunks = owner_ref.shape[0]
    devices = LANES
    number, device = round_ref[0], dev_ref[0]

    def kept(dest):
        shared = jnp.bitwise_and(jnp.bitwise_xor(dest, device), 15) == 0
        return jnp.where(shared, THIRD_ROW, KEPT)

    rows = iota((devices, LANES), 0)
    cols = iota((devices, LANES), 1)
    upto = jnp.where(rows <= cols, 1.0, 0.0).astype(jnp.bfloat16)
    high_half = rows < 64
    rank_of_row = jnp.bitwise_and(rows, 63)
    owner = owner_ref[...]
    box = box_ref[...]
    dest = bits_to(box, [(3 + b, 6 - b) for b in range(7)])
    places = [(0, 9), (1, 8), (2, 7), (4, 6), (5, 5), (3, 4), (6, 3)]
    target = bits_to(owner, places) + jnp.bitwise_and(box, 7) + 1
    target_high = jnp.right_shift(target, 5)
    target_low = jnp.bitwise_and(target, 31)
    count = jnp.zeros((devices, 1), jnp.float32)
    labels = jnp.zeros((devices, LANES), jnp.float32)
    for c in range(chunks):
        dest_c = dest[c : c + 1, :]
        hit = dest_c == rows
        onehot = jnp.where(hit, 1.0, 0.0).astype(jnp.bfloat16)
        upto_here = jnp.dot(onehot, upto, preferred_element_type=jnp.float32) + count
        rank = jnp.sum(jnp.where(hit, upto_here, 0.0), axis=0, keepdims=True) - 1.0
        count = upto_here[:, LANES - 1 : LANES]
        kept_c = kept(dest_c)
        rank = rank.astype(jnp.int32) - number * kept_c
        now = jnp.logical_and(rank >= 0, rank < kept_c)
        slot_vmem[c : c + 1, :] = dest_c * SLOTS + jnp.where(now, rank, LABEL_ROW)
        part = jnp.where(high_half, target_high[c : c + 1, :], target_low[c : c + 1, :])
        part = jnp.where(rank == rank_of_row, part, 0).astype(jnp.float32).astype(jnp.bfloat16)
        labels = labels + lax.dot_general(
            onehot, part, (((1,), (1,)), ((), ())), preferred_element_type=jnp.float32
        )
    copies[4].start()
    copies[2].wait()
    angle_rows = sum(angles_for_all(twiddle_ref, n, lane) for n, lane in enumerate(ANGLE_LANES))
    passes = kept(rows)
    most = jnp.max(count - ((number + 1) * passes[:, :1]).astype(jnp.float32), axis=0, keepdims=True)
    left = jnp.where(most > 0.0, 1.0, 0.0)
    label_rows = labels * 32.0 + pltpu.roll(labels, 64, 1)
    label_rows = jnp.where(cols < passes, label_rows, jnp.where(cols == FLAG_LANE, left, 0.0))
    copies[4].wait()
    copies[3].wait()

    def move(c, carry):
        base = pl.multiple_of(c * LANES, LANES)
        for k in range(LANES):
            out_ref[pl.ds(slot_smem[c, k], 1), :] = src_ref[pl.ds(base + k, 1), :]
        return carry

    lax.fori_loop(0, chunks, move, 0)
    out_ref[pl.ds(LABEL_ROW, devices, stride=SLOTS), :] = label_rows
    out_ref[pl.ds(ANGLE_ROW, devices, stride=SLOTS), :] = angle_rows
    for h in range(8):
        part = 4 * (h & 1) + (h & 2) + (h >> 2)
        out_ref[pl.ds(third_place(device, h), 1), :] = twiddle_ref[
            3:4, part * LANES : (part + 1) * LANES
        ]


def third_place(device, h):
    return ((device & 15) + 16 * h) * SLOTS + THIRD_ROW


def params():
    return pltpu.CompilerParams(vmem_limit_bytes=VMEM_LIMIT)


def in_vmem(count):
    return [pl.BlockSpec(memory_space=pltpu.VMEM)] * count


def anywhere(count):
    return [pl.BlockSpec(memory_space=pl.ANY)] * count


def in_smem():
    return [pl.BlockSpec(memory_space=pltpu.SMEM)]


def pack(number, sources, owner, box, twiddle):
    count, width = sources.shape
    chunks = count // LANES
    block = pltpu.VMEM((chunks, LANES), jnp.int32)
    return pl.pallas_call(
        pack_kernel,
        out_shape=jax.ShapeDtypeStruct((LANES * SLOTS, width), jnp.float32),
        in_specs=in_smem() * 2 + anywhere(4),
        out_specs=in_vmem(1)[0],
        scratch_shapes=[
            block,
            block,
            pltpu.VMEM(twiddle.shape, jnp.float32),
            pltpu.VMEM(sources.shape, jnp.float32),
            block,
            pltpu.SMEM((chunks, LANES), jnp.int32),
            pltpu.SemaphoreType.DMA((5,)),
        ],
        compiler_params=params(),
    )(
        number.reshape(1),
        own_number(),
        owner.reshape(chunks, LANES),
        box.reshape(chunks, LANES),
        twiddle,
        sources,
    )


def deliver(packed):
    width = packed.shape[1]
    return lax.all_to_all(
        packed.reshape(-1, SLOTS, width), ("gx", "gy"), split_axis=0, concat_axis=0, tiled=True
    ).reshape(-1, width)


LAYOUTS = (
    ("e0", "D1", "D2", "D4", "D5", "D3", "D6"),
    ("e0", "e1", "D2", "D4", "D5", "D3", "D6"),
    ("e0", "e1", "e2", "D4", "D5", "D3", "D6"),
    ("D4", "D5", "e3", "e0", "e1", "e2", "D6"),
    ("e4", "D5", "e3", "e0", "e1", "e2", "D6"),
    ("e4", "e5", "e3", "e0", "e1", "e2", "D6"),
    ("e4", "e5", "e6", "e0", "e1", "e2", "e3"),
)
MASKS = 0x1241124
EXCHANGES_TO = 0x743


def twiddle_place(level, position, device):
    names = {}
    for place, name in enumerate(LAYOUTS[level]):
        names[name] = bit(position, 9 - place)
    for b in range(3):
        names["q" + str(b)] = bit(position, b)
    owner = 0
    for b in range(7):
        here = names["D" + str(b)] if b > level else bit(device, b)
        owner = owner + jnp.left_shift(here, b)
    order = [bit(device, b) for b in range(level + 1, 7)]
    order = order + [names["q2"], names["q1"], names["q0"]]
    order = order + [names["e" + str(b)] for b in range(level + 1)]
    index = 0
    for value in order:
        index = index * 2 + value
    return owner, index


def rotations(held, row, column, level, cos_ref, sin_ref):
    pick = jnp.where(row == iota((held.shape[0], 8 * LANES), 0), 1.0, 0.0)
    spread = exact_dot(held, pick, (0, 0))
    mine = column == iota((LANES, 8 * LANES), 0)
    angle = jnp.sum(jnp.where(mine, spread, 0.0), axis=0, keepdims=True)
    angle = jnp.concatenate([angle[:, c * LANES : (c + 1) * LANES] for c in range(8)], axis=0)
    cos_ref[level * 8 : level * 8 + 8, :] = jnp.cos(angle)
    sin_ref[level * 8 : level * 8 + 8, :] = jnp.sin(angle)


def split(value):
    high = value.astype(jnp.bfloat16)
    low = (value - high.astype(jnp.float32)).astype(jnp.bfloat16)
    return high, low


def prepare_kernel(
    dev_ref, twiddle_ref, leaf_ref, ops_ref, cos_ref, sin_ref, leaf_h, leaf_l, mats_h, mats_l
):
    cos_ref[0:48, :] = jnp.zeros((48, LANES), jnp.float32)
    sin_ref[0:48, :] = jnp.zeros((48, LANES), jnp.float32)
    _, index = twiddle_place(6, iota((1, 8 * LANES), 1), dev_ref[0])
    angles = [twiddle_ref[6:7, c * LANES : (c + 1) * LANES] for c in range(8)]
    row, column = jnp.right_shift(index, 7), jnp.bitwise_and(index, LANES - 1)
    rotations(jnp.concatenate(angles, axis=0), row, column, 6, cos_ref, sin_ref)

    def block(real, imag):
        top = jnp.concatenate([real, imag], axis=1)
        bottom = jnp.concatenate([-imag, real], axis=1)
        return jnp.concatenate([top, bottom], axis=0).T

    leaf = block(leaf_ref[0], leaf_ref[1])
    leaf_h[...], leaf_l[...] = split(leaf)

    def build(n, carry):
        level, e, c = n // 4, lax.rem(n, 4) // 2, lax.rem(n, 2)
        high, low = split(block(ops_ref[level, e, c, 0], ops_ref[level, e, c, 1]))
        out = pl.ds(pl.multiple_of(e * LANES, LANES), LANES)
        across = pl.ds(pl.multiple_of(c * LANES, LANES), LANES)
        mats_h[level, out, across] = high
        mats_l[level, out, across] = low
        return carry

    lax.fori_loop(0, 4 * ops_ref.shape[0], build, 0, unroll=2)


def prepare(twiddle, leaf_op, level_ops):
    levels, count = twiddle.shape
    width = 2 * leaf_op.shape[1]
    return pl.pallas_call(
        prepare_kernel,
        out_shape=[
            jax.ShapeDtypeStruct((levels * count // LANES, LANES), jnp.float32),
            jax.ShapeDtypeStruct((levels * count // LANES, LANES), jnp.float32),
            jax.ShapeDtypeStruct((width, width), jnp.bfloat16),
            jax.ShapeDtypeStruct((width, width), jnp.bfloat16),
            jax.ShapeDtypeStruct((levels, 2 * width, 2 * width), jnp.bfloat16),
            jax.ShapeDtypeStruct((levels, 2 * width, 2 * width), jnp.bfloat16),
        ],
        in_specs=in_smem() + in_vmem(3),
        out_specs=in_vmem(6),
        compiler_params=params(),
    )(own_number(), twiddle, leaf_op, level_ops)


def own_number():
    device = lax.axis_index("gx") * lax.axis_size("gy") + lax.axis_index("gy")
    return device.reshape(1).astype(jnp.int32)


def product(high, low, value):
    value_high, value_low = split(value)
    total = jnp.dot(high, value_high, preferred_element_type=jnp.float32)
    total += jnp.dot(high, value_low, preferred_element_type=jnp.float32)
    total += jnp.dot(low, value_high, preferred_element_type=jnp.float32)
    return total


def moved_rotations(angles, third, peers, device, cos_ref, sin_ref):
    position = iota((1, 8 * LANES), 1)
    for level in range(6):
        owner, index = twiddle_place(level, position, device)
        if level < 3:
            held, row = angles, owner
            column = ANGLE_LANES[level] + jnp.bitwise_and(index, (16 << level) - 1)
        elif level == 3:
            held, row = third, jnp.right_shift(owner, 4)
            column = jnp.bitwise_and(index, LANES - 1)
        else:
            taken = 2 ** (level - 3)
            fixed = 0
            for b in range(level + 1, 7):
                fixed = fixed * 2 + bit(device, b)
            parts = []
            for k in range(taken):
                lane = pl.multiple_of((fixed * taken + k) * LANES, LANES)
                parts += [peer[level : level + 1, pl.ds(lane, LANES)] for peer in peers]
            held = jnp.concatenate(parts, axis=0)
            row = jnp.right_shift(jnp.bitwise_xor(owner, device), 5)
            row = row + 4 * jnp.bitwise_and(jnp.right_shift(index, 7), taken - 1)
            column = jnp.bitwise_and(index, LANES - 1)
        rotations(held, row, column, level, cos_ref, sin_ref)


def third_angles(x_ref, device):
    rows = [x_ref[pl.ds(third_place(device, h), 1), :] for h in range(8)]
    return jnp.concatenate(rows, axis=0)


def add_rows(x_ref, names, first, count):
    ranks = [first + k for k in range(count)]
    value = jnp.concatenate([x_ref[pl.ds(r, LANES, stride=SLOTS), :] for r in ranks], axis=0)
    name = jnp.concatenate([names[pl.ds(r, 1), :] for r in ranks], axis=1)
    targets = iota((8 * LANES, count * LANES), 0).astype(jnp.float32)
    pick = jnp.where(targets == name, 1.0, 0.0).astype(jnp.bfloat16)
    both = jnp.concatenate(split(value), axis=1)
    return jnp.dot(pick, both, preferred_element_type=jnp.float32)


def chunk_pairs(mask):
    lows = [2 * n - (n & (mask - 1)) for n in range(4)]
    return [(low, low + mask) for low in lows]


def nibble(table, n):
    return (table >> (4 * n)) & 15


def exchange(state, mask, weight):
    lane_set = jnp.bitwise_and(iota((LANES, LANES), 1), weight) != 0
    out = list(state)
    for low, high in chunk_pairs(mask):
        lower, upper = state[low], state[high]
        out[low] = jnp.where(lane_set, pltpu.roll(upper, weight, 1), lower)
        out[high] = jnp.where(lane_set, upper, pltpu.roll(lower, LANES - weight, 1))
    return out


def butterfly(state, mask, high, low, cos_ref, sin_ref, number):
    half = LANES // 2
    stacked = jnp.concatenate(
        [jnp.concatenate([state[pair[c]] for pair in chunk_pairs(mask)], axis=1) for c in range(2)],
        axis=0,
    )
    mixed = product(high, low, stacked)
    out = list(state)
    for n, pair in enumerate(chunk_pairs(mask)):
        for e in range(2):
            block = mixed[e * LANES : (e + 1) * LANES, n * LANES : (n + 1) * LANES]
            real, imag = block[:half], block[half:]
            place = number * 8 + pair[e]
            cosine = cos_ref[place : place + 1, :]
            sine = sin_ref[place : place + 1, :]
            out[pair[e]] = jnp.concatenate(
                [real * cosine - imag * sine, real * sine + imag * cosine], axis=0
            )
    return out


def finish_kernel(
    dev_ref, x_ref, peer0, peer1, peer2, peer3,
    cos_in, sin_in, leaf_h_in, leaf_l_in, mats_h_in, mats_l_in, out_ref, flag_ref,
    sums, names, cos_ref, sin_ref, cos_far, sin_far, leaf_h, leaf_l, mats_h, mats_l, sems,
):
    pairs = (
        (cos_in, cos_far), (sin_in, sin_far), (leaf_h_in, leaf_h), (leaf_l_in, leaf_l),
        (mats_h_in, mats_h), (mats_l_in, mats_l),
    )
    copies = [pltpu.make_async_copy(a, b, sems.at[n]) for n, (a, b) in enumerate(pairs)]
    for copy in copies:
        copy.start()
    labels = x_ref[pl.ds(LABEL_ROW, LANES, stride=SLOTS), :]
    names[...] = labels.T - 1.0
    flag_ref[0] = jnp.max(names[FLAG_LANE : FLAG_LANE + 1, :] + 1.0).astype(jnp.int32)
    column = iota((LANES, LANES), 1)
    filled = jnp.logical_and(labels > 0.0, column < KEPT)
    most = jnp.max(jnp.where(filled, column + 1, 0).astype(jnp.float32)).astype(jnp.int32)
    sums[...] = add_rows(x_ref, names, 0, SURE)
    angles = x_ref[pl.ds(ANGLE_ROW, LANES, stride=SLOTS), :]
    third = third_angles(x_ref, dev_ref[0])
    peers = (peer0, peer1, peer2, peer3)
    moved_rotations(angles, third, peers, dev_ref[0], cos_ref, sin_ref)
    for first in range(SURE, SLOTS, STEP):

        @pl.when(most > first)
        def _():
            sums[...] += add_rows(x_ref, names, first, STEP)

    for copy in copies:
        copy.wait()
    cos_ref[48:, :] = cos_far[48:, :]
    sin_ref[48:, :] = sin_far[48:, :]
    state = []
    for c in range(8):
        block = sums[c * LANES : (c + 1) * LANES, :]
        state.append((block[:, :LANES] + block[:, LANES:]).T)
    leafed = product(leaf_h[...], leaf_l[...], jnp.concatenate(state, axis=1))
    state = [leafed[:, c * LANES : (c + 1) * LANES] for c in range(8)]
    done = 0
    for number in range(7):
        mask = nibble(MASKS, number)
        state = butterfly(state, mask, mats_h[number], mats_l[number], cos_ref, sin_ref, number)
        if number in (2, 5, 6):
            then = nibble(EXCHANGES_TO, number // 3)
            for n in range(done, then):
                state = exchange(state, nibble(MASKS, n), LANES // 2 >> n)
            done = then
    for c in range(8):
        out_ref[c * LANES : (c + 1) * LANES, :] = state[c].T


def finish(arrived, peers, prepared, box_count):
    width = arrived.shape[1]
    table = pltpu.VMEM(prepared[0].shape, jnp.float32)
    return pl.pallas_call(
        finish_kernel,
        out_shape=[
            jax.ShapeDtypeStruct((box_count, width), jnp.float32),
            jax.ShapeDtypeStruct((1,), jnp.int32),
        ],
        in_specs=in_smem() + in_vmem(5) + anywhere(6),
        out_specs=in_vmem(1) + in_smem(),
        scratch_shapes=[
            pltpu.VMEM((box_count, 2 * width), jnp.float32),
            pltpu.VMEM((LANES, LANES), jnp.float32),
            table,
            table,
        ]
        + [pltpu.VMEM(array.shape, array.dtype) for array in prepared]
        + [pltpu.SemaphoreType.DMA((len(prepared),))],
        compiler_params=params(),
    )(own_number(), arrived, *peers, *prepared)


def collect_kernel(dev_ref, x_ref, before_ref, sums, angle_ref, flag_ref, names):
    labels = x_ref[pl.ds(LABEL_ROW, LANES, stride=SLOTS), :]
    angle_ref[:LANES, :] = x_ref[pl.ds(ANGLE_ROW, LANES, stride=SLOTS), :]
    angle_ref[LANES:, :] = third_angles(x_ref, dev_ref[0])
    names[...] = labels.T - 1.0
    flag_ref[0] = jnp.max(names[FLAG_LANE : FLAG_LANE + 1, :] + 1.0).astype(jnp.int32)
    names[FLAG_LANE : FLAG_LANE + 1, :] = jnp.full((1, LANES), -1.0)
    sums[...] = before_ref[...]

    def body(pair, carry):
        sums[...] += add_rows(x_ref, names, 2 * pair, 2)
        return carry

    lax.fori_loop(0, SLOTS // 2, body, 0)


def collect(arrived, sums):
    return pl.pallas_call(
        collect_kernel,
        out_shape=[
            jax.ShapeDtypeStruct(sums.shape, jnp.float32),
            jax.ShapeDtypeStruct((LANES + 8, LANES), jnp.float32),
            jax.ShapeDtypeStruct((1,), jnp.int32),
        ],
        in_specs=in_smem() + in_vmem(2),
        out_specs=in_vmem(2) + in_smem(),
        scratch_shapes=[pltpu.VMEM((LANES, LANES), jnp.float32)],
        compiler_params=params(),
    )(own_number(), arrived, sums)


def levels_kernel(
    dev_ref, sums, angles_ref, peer0, peer1, peer2, peer3, cos_in, sin_in, leaf_h, leaf_l, mats_h, mats_l,
    out_ref, state, cos_ref, sin_ref,
):
    half = LANES // 2
    cos_ref[...] = cos_in[...]
    sin_ref[...] = sin_in[...]
    angles, third = angles_ref[:LANES, :], angles_ref[LANES:, :]
    peers = (peer0, peer1, peer2, peer3)
    moved_rotations(angles, third, peers, dev_ref[0], cos_ref, sin_ref)

    def leaf(c, carry):
        block = sums[pl.ds(pl.multiple_of(c * LANES, LANES), LANES), :]
        state[c] = product(leaf_h[...], leaf_l[...], (block[:, :LANES] + block[:, LANES:]).T)
        return carry

    lax.fori_loop(0, 8, leaf, 0)

    def level(number, carry):
        pairs = chunk_pairs(nibble(MASKS, number))
        stacked = jnp.concatenate(
            [jnp.concatenate([state[pair[c]] for pair in pairs], axis=1) for c in range(2)], axis=0
        )
        mixed = product(mats_h[number], mats_l[number], stacked)
        for n, pair in enumerate(pairs):
            for e in range(2):
                block = mixed[e * LANES : (e + 1) * LANES, n * LANES : (n + 1) * LANES]
                real, imag = block[:half], block[half:]
                cosine = cos_ref[pl.ds(number * 8 + pair[e], 1), :]
                sine = sin_ref[pl.ds(number * 8 + pair[e], 1), :]
                state[pair[e], :half, :] = real * cosine - imag * sine
                state[pair[e], half:, :] = real * sine + imag * cosine
        return carry

    def swap(number, carry):
        weight = half >> number
        lane_set = jnp.bitwise_and(iota((LANES, LANES), 1), weight) != 0
        for low, high in chunk_pairs(nibble(MASKS, number)):
            lower, upper = state[low], state[high]
            state[low] = jnp.where(lane_set, pltpu.roll(upper, weight, 1), lower)
            state[high] = jnp.where(lane_set, upper, pltpu.roll(lower, LANES - weight, 1))
        return carry

    def phase(number, done):
        lax.fori_loop(3 * number, jnp.minimum(3 * number + 3, 7), level, 0)
        then = nibble(EXCHANGES_TO, number)
        lax.fori_loop(done, then, swap, 0)
        return then

    lax.fori_loop(0, 3, phase, 0)

    def write(c, carry):
        out_ref[pl.ds(pl.multiple_of(c * LANES, LANES), LANES), :] = state[c].T
        return carry

    lax.fori_loop(0, 8, write, 0)


def transform(sums, angles, peers, prepared):
    box_count, width = sums.shape[0], sums.shape[1] // 2
    table = pltpu.VMEM(prepared[0].shape, jnp.float32)
    return pl.pallas_call(
        levels_kernel,
        out_shape=jax.ShapeDtypeStruct((box_count, width), jnp.float32),
        in_specs=in_smem() + in_vmem(12),
        out_specs=in_vmem(1)[0],
        scratch_shapes=[pltpu.VMEM((8, width, LANES), jnp.float32), table, table],
        compiler_params=params(),
    )(own_number(), sums, angles, *peers, *prepared)


def in_rounds(sources, owner, box, peers, prepared):
    twiddle = peers[0]
    box_count, width = twiddle.shape[1], sources.shape[1]

    def body(carry):
        number, sums, _, _ = carry
        arrived = deliver(pack(number, sources, owner, box, twiddle))
        return (number + 1, *collect(arrived, sums))

    start = (
        jnp.int32(0),
        jnp.zeros((box_count, 2 * width), jnp.float32),
        jnp.zeros((LANES + 8, LANES), jnp.float32),
        jnp.ones((1,), jnp.int32),
    )
    _, sums, angles, _ = lax.while_loop(lambda carry: carry[3][0] > 0, body, start)
    return transform(sums, angles, peers, prepared)


def local(sources, owner, box, leaf_op, level_ops, twiddle):
    box_count = twiddle.shape[1]
    packed = pack(jnp.int32(0), sources, owner, box, twiddle)
    arrived = deliver(packed)
    peers = [twiddle] + [swapped(twiddle, "gx", 4 * i) for i in range(1, 4)]
    prepared = prepare(twiddle, leaf_op, level_ops)
    blocks, flag = finish(arrived, peers, prepared, box_count)
    return lax.cond(
        flag[0] > 0,
        lambda: in_rounds(sources, owner, box, peers, prepared),
        lambda: blocks,
    )


def solution(mesh):
    in_specs = (
        P(("gx", "gy"), None),
        P(("gx", "gy"), None),
        P(("gx", "gy")),
        P(),
        P(),
        P(None, ("gx", "gy")),
    )
    out_specs = P(("gx", "gy"), None)
    return jax.shard_map(local, mesh=mesh, in_specs=in_specs, out_specs=out_specs, check_vma=False)
```

```python
import jax
import jax.numpy as jnp
from jax import lax
from jax.experimental import pallas as pl
from jax.experimental.pallas import tpu as pltpu
from jax.sharding import PartitionSpec as P

LANES = 128
VMEM_LIMIT = 48 * 1024 * 1024


def swapped(shard, axis, shift):
    return lax.ppermute(shard, axis, [(i, i ^ shift) for i in range(lax.axis_size(axis))])


SLOTS = 40
KEPT = SLOTS - 2
LABEL_ROW = KEPT
FLAG_LANE = KEPT
ANGLE_ROW = KEPT + 1
ANGLE_LANES = (0, 32, 64)
THIRD_ROW = KEPT - 1
SURE = 16
STEP = 4


def bit(value, place):
    return jnp.bitwise_and(jnp.right_shift(value, place), 1)


def bits_to(value, places):
    total = None
    for source, target in places:
        term = jnp.left_shift(bit(value, source), target)
        total = term if total is None else total + term
    return total


def iota(shape, axis):
    return lax.broadcasted_iota(jnp.int32, shape, axis)


def exact_dot(left, right, contract=(1, 0)):
    return lax.dot_general(
        left,
        right,
        (((contract[0],), (contract[1],)), ((), ())),
        precision=lax.Precision.HIGHEST,
        preferred_element_type=jnp.float32,
    )


def angles_for_all(twiddle_ref, level, lane):
    width = 16 << level
    devices = LANES
    dest = iota((devices, LANES), 0)
    cols = iota((devices, LANES), 1)
    first = bits_to(dest, [(level + 1 + b, 2 - b) for b in range(3)])
    last = range(level + 4, 7)
    group = bits_to(dest, [(b, 6 - b) for b in last])
    rows = jnp.zeros((devices, LANES), jnp.float32)
    for g in range(8):
        part = twiddle_ref[level : level + 1, g * LANES : (g + 1) * LANES]
        rows = jnp.where(first == g, part, rows)
    rows = jnp.where(jnp.right_shift(cols, 4 + level) == group, rows, 0.0)
    fold = jnp.where(cols == lane + jnp.bitwise_and(dest, width - 1), 1.0, 0.0)
    return exact_dot(rows, fold)


def pack_kernel(
    round_ref, dev_ref, owner_hbm, box_hbm, twiddle_hbm, src_hbm, out_ref,
    owner_ref, box_ref, twiddle_ref, src_ref, slot_vmem, slot_smem, sems,
):
    pairs = (
        (owner_hbm, owner_ref), (box_hbm, box_ref), (twiddle_hbm, twiddle_ref), (src_hbm, src_ref),
        (slot_vmem, slot_smem),
    )
    copies = [pltpu.make_async_copy(a, b, sems.at[n]) for n, (a, b) in enumerate(pairs)]
    for copy in copies[:4]:
        copy.start()

    def clear(n, carry):
        out_ref[pl.ds(pl.multiple_of(n * 64, 64), 64), :] = jnp.zeros((64, LANES), jnp.float32)
        return carry

    lax.fori_loop(0, out_ref.shape[0] // 64, clear, 0)
    copies[0].wait()
    copies[1].wait()
    chunks = owner_ref.shape[0]
    devices = LANES
    number, device = round_ref[0], dev_ref[0]

    def kept(dest):
        shared = jnp.bitwise_and(jnp.bitwise_xor(dest, device), 15) == 0
        return jnp.where(shared, THIRD_ROW, KEPT)

    rows = iota((devices, LANES), 0)
    cols = iota((devices, LANES), 1)
    upto = jnp.where(rows <= cols, 1.0, 0.0).astype(jnp.bfloat16)
    high_half = rows < 64
    rank_of_row = jnp.bitwise_and(rows, 63)
    owner = owner_ref[...]
    box = box_ref[...]
    dest = bits_to(box, [(3 + b, 6 - b) for b in range(7)])
    places = [(0, 9), (1, 8), (2, 7), (4, 6), (5, 5), (3, 4), (6, 3)]
    target = bits_to(owner, places) + jnp.bitwise_and(box, 7) + 1
    target_high = jnp.right_shift(target, 5)
    target_low = jnp.bitwise_and(target, 31)
    count = jnp.zeros((devices, 1), jnp.float32)
    labels = jnp.zeros((devices, LANES), jnp.float32)
    for c in range(chunks):
        dest_c = dest[c : c + 1, :]
        hit = dest_c == rows
        onehot = jnp.where(hit, 1.0, 0.0).astype(jnp.bfloat16)
        upto_here = jnp.dot(onehot, upto, preferred_element_type=jnp.float32) + count
        rank = jnp.sum(jnp.where(hit, upto_here, 0.0), axis=0, keepdims=True) - 1.0
        count = upto_here[:, LANES - 1 : LANES]
        kept_c = kept(dest_c)
        rank = rank.astype(jnp.int32) - number * kept_c
        now = jnp.logical_and(rank >= 0, rank < kept_c)
        slot_vmem[c : c + 1, :] = dest_c * SLOTS + jnp.where(now, rank, LABEL_ROW)
        part = jnp.where(high_half, target_high[c : c + 1, :], target_low[c : c + 1, :])
        part = jnp.where(rank == rank_of_row, part, 0).astype(jnp.float32).astype(jnp.bfloat16)
        labels = labels + lax.dot_general(
            onehot, part, (((1,), (1,)), ((), ())), preferred_element_type=jnp.float32
        )
    copies[4].start()
    copies[2].wait()
    angle_rows = sum(angles_for_all(twiddle_ref, n, lane) for n, lane in enumerate(ANGLE_LANES))
    passes = kept(rows)
    most = jnp.max(count - ((number + 1) * passes[:, :1]).astype(jnp.float32), axis=0, keepdims=True)
    left = jnp.where(most > 0.0, 1.0, 0.0)
    label_rows = labels * 32.0 + pltpu.roll(labels, 64, 1)
    label_rows = jnp.where(cols < passes, label_rows, jnp.where(cols == FLAG_LANE, left, 0.0))
    copies[4].wait()
    copies[3].wait()

    def move(c, carry):
        base = pl.multiple_of(c * LANES, LANES)
        for k in range(LANES):
            out_ref[pl.ds(slot_smem[c, k], 1), :] = src_ref[pl.ds(base + k, 1), :]
        return carry

    lax.fori_loop(0, chunks, move, 0)
    out_ref[pl.ds(LABEL_ROW, devices, stride=SLOTS), :] = label_rows
    out_ref[pl.ds(ANGLE_ROW, devices, stride=SLOTS), :] = angle_rows
    for h in range(8):
        part = 4 * (h & 1) + (h & 2) + (h >> 2)
        out_ref[pl.ds(third_place(device, h), 1), :] = twiddle_ref[
            3:4, part * LANES : (part + 1) * LANES
        ]


def third_place(device, h):
    return ((device & 15) + 16 * h) * SLOTS + THIRD_ROW


def params():
    return pltpu.CompilerParams(vmem_limit_bytes=VMEM_LIMIT)


def in_vmem(count):
    return [pl.BlockSpec(memory_space=pltpu.VMEM)] * count


def anywhere(count):
    return [pl.BlockSpec(memory_space=pl.ANY)] * count


def in_smem():
    return [pl.BlockSpec(memory_space=pltpu.SMEM)]


def pack(number, sources, owner, box, twiddle):
    count, width = sources.shape
    chunks = count // LANES
    block = pltpu.VMEM((chunks, LANES), jnp.int32)
    return pl.pallas_call(
        pack_kernel,
        out_shape=jax.ShapeDtypeStruct((LANES * SLOTS, width), jnp.float32),
        in_specs=in_smem() * 2 + anywhere(4),
        out_specs=in_vmem(1)[0],
        scratch_shapes=[
            block,
            block,
            pltpu.VMEM(twiddle.shape, jnp.float32),
            pltpu.VMEM(sources.shape, jnp.float32),
            block,
            pltpu.SMEM((chunks, LANES), jnp.int32),
            pltpu.SemaphoreType.DMA((5,)),
        ],
        compiler_params=params(),
    )(
        number.reshape(1),
        own_number(),
        owner.reshape(chunks, LANES),
        box.reshape(chunks, LANES),
        twiddle,
        sources,
    )


def deliver(packed):
    width = packed.shape[1]
    return lax.all_to_all(
        packed.reshape(-1, SLOTS, width), ("gx", "gy"), split_axis=0, concat_axis=0, tiled=True
    ).reshape(-1, width)


LAYOUTS = (
    ("e0", "D1", "D2", "D4", "D5", "D3", "D6"),
    ("e0", "e1", "D2", "D4", "D5", "D3", "D6"),
    ("e0", "e1", "e2", "D4", "D5", "D3", "D6"),
    ("D4", "D5", "e3", "e0", "e1", "e2", "D6"),
    ("e4", "D5", "e3", "e0", "e1", "e2", "D6"),
    ("e4", "e5", "e3", "e0", "e1", "e2", "D6"),
    ("e4", "e5", "e6", "e0", "e1", "e2", "e3"),
)
MASKS = 0x1241124
EXCHANGES_TO = 0x743


def twiddle_place(level, position, device):
    names = {}
    for place, name in enumerate(LAYOUTS[level]):
        names[name] = bit(position, 9 - place)
    for b in range(3):
        names["q" + str(b)] = bit(position, b)
    owner = 0
    for b in range(7):
        here = names["D" + str(b)] if b > level else bit(device, b)
        owner = owner + jnp.left_shift(here, b)
    order = [bit(device, b) for b in range(level + 1, 7)]
    order = order + [names["q2"], names["q1"], names["q0"]]
    order = order + [names["e" + str(b)] for b in range(level + 1)]
    index = 0
    for value in order:
        index = index * 2 + value
    return owner, index


def picked(held, row, column):
    pick = jnp.where(row == iota((held.shape[0], 8 * LANES), 0), 1.0, 0.0).astype(jnp.bfloat16)
    high = held.astype(jnp.bfloat16)
    rest = held - high.astype(jnp.float32)
    parts = (high, *split(rest))
    spread = sum(
        lax.dot_general(part, pick, (((0,), (0,)), ((), ())), preferred_element_type=jnp.float32)
        for part in parts
    )
    mine = column == iota((LANES, 8 * LANES), 0)
    angle = jnp.sum(jnp.where(mine, spread, 0.0), axis=0, keepdims=True)
    return jnp.concatenate([angle[:, c * LANES : (c + 1) * LANES] for c in range(8)], axis=0)


def split(value):
    high = value.astype(jnp.bfloat16)
    low = (value - high.astype(jnp.float32)).astype(jnp.bfloat16)
    return high, low


def prepare_kernel(
    dev_ref, twiddle_ref, leaf_ref, ops_ref, cos_ref, sin_ref, leaf_h, leaf_l, mats_h, mats_l
):
    cos_ref[0:48, :] = jnp.zeros((48, LANES), jnp.float32)
    sin_ref[0:48, :] = jnp.zeros((48, LANES), jnp.float32)
    _, index = twiddle_place(6, iota((1, 8 * LANES), 1), dev_ref[0])
    angles = [twiddle_ref[6:7, c * LANES : (c + 1) * LANES] for c in range(8)]
    row, column = jnp.right_shift(index, 7), jnp.bitwise_and(index, LANES - 1)
    angle = picked(jnp.concatenate(angles, axis=0), row, column)
    cos_ref[48:56, :] = jnp.cos(angle)
    sin_ref[48:56, :] = jnp.sin(angle)

    def block(real, imag):
        top = jnp.concatenate([real, imag], axis=1)
        bottom = jnp.concatenate([-imag, real], axis=1)
        return jnp.concatenate([top, bottom], axis=0).T

    leaf = block(leaf_ref[0], leaf_ref[1])
    leaf_h[...], leaf_l[...] = split(leaf)

    def build(n, carry):
        level, e, c = n // 4, lax.rem(n, 4) // 2, lax.rem(n, 2)
        high, low = split(block(ops_ref[level, e, c, 0], ops_ref[level, e, c, 1]))
        out = pl.ds(pl.multiple_of(e * LANES, LANES), LANES)
        across = pl.ds(pl.multiple_of(c * LANES, LANES), LANES)
        mats_h[level, out, across] = high
        mats_l[level, out, across] = low
        return carry

    lax.fori_loop(0, 4 * ops_ref.shape[0], build, 0, unroll=2)


def prepare(twiddle, leaf_op, level_ops):
    levels, count = twiddle.shape
    width = 2 * leaf_op.shape[1]
    return pl.pallas_call(
        prepare_kernel,
        out_shape=[
            jax.ShapeDtypeStruct((levels * count // LANES, LANES), jnp.float32),
            jax.ShapeDtypeStruct((levels * count // LANES, LANES), jnp.float32),
            jax.ShapeDtypeStruct((width, width), jnp.bfloat16),
            jax.ShapeDtypeStruct((width, width), jnp.bfloat16),
            jax.ShapeDtypeStruct((levels, 2 * width, 2 * width), jnp.bfloat16),
            jax.ShapeDtypeStruct((levels, 2 * width, 2 * width), jnp.bfloat16),
        ],
        in_specs=in_smem() + in_vmem(3),
        out_specs=in_vmem(6),
        compiler_params=params(),
    )(own_number(), twiddle, leaf_op, level_ops)


def own_number():
    device = lax.axis_index("gx") * lax.axis_size("gy") + lax.axis_index("gy")
    return device.reshape(1).astype(jnp.int32)


def product(high, low, value):
    value_high, value_low = split(value)
    total = jnp.dot(high, value_high, preferred_element_type=jnp.float32)
    total += jnp.dot(high, value_low, preferred_element_type=jnp.float32)
    total += jnp.dot(low, value_high, preferred_element_type=jnp.float32)
    return total


def moved_rotations(angles, third, peers, device, cos_ref, sin_ref):
    position = iota((1, 8 * LANES), 1)
    angle = []
    for level in range(6):
        owner, index = twiddle_place(level, position, device)
        if level < 3:
            held, row = angles, owner
            column = ANGLE_LANES[level] + jnp.bitwise_and(index, (16 << level) - 1)
        elif level == 3:
            held, row = third, jnp.right_shift(owner, 4)
            column = jnp.bitwise_and(index, LANES - 1)
        else:
            taken = 2 ** (level - 3)
            fixed = 0
            for b in range(level + 1, 7):
                fixed = fixed * 2 + bit(device, b)
            parts = []
            for k in range(taken):
                lane = pl.multiple_of((fixed * taken + k) * LANES, LANES)
                parts += [peer[level : level + 1, pl.ds(lane, LANES)] for peer in peers]
            held = jnp.concatenate(parts, axis=0)
            row = jnp.right_shift(jnp.bitwise_xor(owner, device), 5)
            row = row + 4 * jnp.bitwise_and(jnp.right_shift(index, 7), taken - 1)
            column = jnp.bitwise_and(index, LANES - 1)
        angle.append(picked(held, row, column))
    angle = jnp.concatenate(angle, axis=0)
    cos_ref[0:48, :] = jnp.cos(angle)
    sin_ref[0:48, :] = jnp.sin(angle)


def third_angles(x_ref, device):
    rows = [x_ref[pl.ds(third_place(device, h), 1), :] for h in range(8)]
    return jnp.concatenate(rows, axis=0)


def add_rows(x_ref, names, first, count):
    ranks = [first + k for k in range(count)]
    value = jnp.concatenate([x_ref[pl.ds(r, LANES, stride=SLOTS), :] for r in ranks], axis=0)
    name = jnp.concatenate([names[pl.ds(r, 1), :] for r in ranks], axis=1)
    targets = iota((8 * LANES, count * LANES), 0).astype(jnp.float32)
    pick = jnp.where(targets == name, 1.0, 0.0).astype(jnp.bfloat16)
    both = jnp.concatenate(split(value), axis=1)
    return jnp.dot(pick, both, preferred_element_type=jnp.float32)


def chunk_pairs(mask):
    lows = [2 * n - (n & (mask - 1)) for n in range(4)]
    return [(low, low + mask) for low in lows]


def nibble(table, n):
    return (table >> (4 * n)) & 15


def exchange(state, mask, weight):
    lane_set = jnp.bitwise_and(iota((LANES, LANES), 1), weight) != 0
    out = list(state)
    for low, high in chunk_pairs(mask):
        lower, upper = state[low], state[high]
        out[low] = jnp.where(lane_set, pltpu.roll(upper, weight, 1), lower)
        out[high] = jnp.where(lane_set, upper, pltpu.roll(lower, LANES - weight, 1))
    return out


def butterfly(state, mask, high, low, cos_ref, sin_ref, number):
    half = LANES // 2
    stacked = jnp.concatenate(
        [jnp.concatenate([state[pair[c]] for pair in chunk_pairs(mask)], axis=1) for c in range(2)],
        axis=0,
    )
    mixed = product(high, low, stacked)
    out = list(state)
    for n, pair in enumerate(chunk_pairs(mask)):
        for e in range(2):
            block = mixed[e * LANES : (e + 1) * LANES, n * LANES : (n + 1) * LANES]
            real, imag = block[:half], block[half:]
            place = number * 8 + pair[e]
            cosine = cos_ref[place : place + 1, :]
            sine = sin_ref[place : place + 1, :]
            out[pair[e]] = jnp.concatenate(
                [real * cosine - imag * sine, real * sine + imag * cosine], axis=0
            )
    return out


def finish_kernel(
    dev_ref, x_ref, peer0, peer1, peer2, peer3,
    cos_in, sin_in, leaf_h_in, leaf_l_in, mats_h_in, mats_l_in,
    out_ref, flag_ref, cos_ref, sin_ref,
    sums, names, cos_far, sin_far, leaf_h, leaf_l, mats_h, mats_l, sems,
):
    pairs = (
        (cos_in, cos_far), (sin_in, sin_far), (leaf_h_in, leaf_h), (leaf_l_in, leaf_l),
        (mats_h_in, mats_h), (mats_l_in, mats_l),
    )
    copies = [pltpu.make_async_copy(a, b, sems.at[n]) for n, (a, b) in enumerate(pairs)]
    for copy in copies:
        copy.start()
    labels = x_ref[pl.ds(LABEL_ROW, LANES, stride=SLOTS), :]
    names[...] = labels.T - 1.0
    flag_ref[0] = jnp.max(names[FLAG_LANE : FLAG_LANE + 1, :] + 1.0).astype(jnp.int32)
    column = iota((LANES, LANES), 1)
    filled = jnp.logical_and(labels > 0.0, column < KEPT)
    most = jnp.max(jnp.where(filled, column + 1, 0).astype(jnp.float32)).astype(jnp.int32)
    sums[...] = add_rows(x_ref, names, 0, SURE)
    angles = x_ref[pl.ds(ANGLE_ROW, LANES, stride=SLOTS), :]
    third = third_angles(x_ref, dev_ref[0])
    peers = (peer0, peer1, peer2, peer3)
    moved_rotations(angles, third, peers, dev_ref[0], cos_ref, sin_ref)
    for first in range(SURE, SLOTS, STEP):

        @pl.when(most > first)
        def _():
            sums[...] += add_rows(x_ref, names, first, STEP)

    for copy in copies:
        copy.wait()
    cos_ref[48:, :] = cos_far[48:, :]
    sin_ref[48:, :] = sin_far[48:, :]
    state = []
    for c in range(8):
        block = sums[c * LANES : (c + 1) * LANES, :]
        state.append((block[:, :LANES] + block[:, LANES:]).T)
    leafed = product(leaf_h[...], leaf_l[...], jnp.concatenate(state, axis=1))
    state = [leafed[:, c * LANES : (c + 1) * LANES] for c in range(8)]
    done = 0
    for number in range(7):
        mask = nibble(MASKS, number)
        state = butterfly(state, mask, mats_h[number], mats_l[number], cos_ref, sin_ref, number)
        if number in (2, 5, 6):
            then = nibble(EXCHANGES_TO, number // 3)
            for n in range(done, then):
                state = exchange(state, nibble(MASKS, n), LANES // 2 >> n)
            done = then
    for c in range(8):
        out_ref[c * LANES : (c + 1) * LANES, :] = state[c].T


def finish(arrived, peers, prepared, box_count):
    width = arrived.shape[1]
    table = jax.ShapeDtypeStruct(prepared[0].shape, jnp.float32)
    return pl.pallas_call(
        finish_kernel,
        out_shape=[
            jax.ShapeDtypeStruct((box_count, width), jnp.float32),
            jax.ShapeDtypeStruct((1,), jnp.int32),
            table,
            table,
        ],
        in_specs=in_smem() + in_vmem(5) + anywhere(6),
        out_specs=in_vmem(1) + in_smem() + in_vmem(2),
        scratch_shapes=[
            pltpu.VMEM((box_count, 2 * width), jnp.float32),
            pltpu.VMEM((LANES, LANES), jnp.float32),
        ]
        + [pltpu.VMEM(array.shape, array.dtype) for array in prepared]
        + [pltpu.SemaphoreType.DMA((len(prepared),))],
        compiler_params=params(),
    )(own_number(), arrived, *peers, *prepared)


def collect_kernel(x_ref, before_ref, sums, flag_ref, names):
    labels = x_ref[pl.ds(LABEL_ROW, LANES, stride=SLOTS), :]
    names[...] = labels.T - 1.0
    flag_ref[0] = jnp.max(names[FLAG_LANE : FLAG_LANE + 1, :] + 1.0).astype(jnp.int32)
    names[FLAG_LANE : FLAG_LANE + 1, :] = jnp.full((1, LANES), -1.0)
    sums[...] = before_ref[...]

    def body(pair, carry):
        sums[...] += add_rows(x_ref, names, 2 * pair, 2)
        return carry

    lax.fori_loop(0, SLOTS // 2, body, 0)


def collect(arrived, sums):
    return pl.pallas_call(
        collect_kernel,
        out_shape=[
            jax.ShapeDtypeStruct(sums.shape, jnp.float32),
            jax.ShapeDtypeStruct((1,), jnp.int32),
        ],
        in_specs=in_vmem(2),
        out_specs=in_vmem(1) + in_smem(),
        scratch_shapes=[pltpu.VMEM((LANES, LANES), jnp.float32)],
        compiler_params=params(),
    )(arrived, sums)


def levels_kernel(sums, cos_ref, sin_ref, leaf_h, leaf_l, mats_h, mats_l, out_ref, state):
    half = LANES // 2

    def leaf(c, carry):
        block = sums[pl.ds(pl.multiple_of(c * LANES, LANES), LANES), :]
        state[c] = product(leaf_h[...], leaf_l[...], (block[:, :LANES] + block[:, LANES:]).T)
        return carry

    lax.fori_loop(0, 8, leaf, 0)

    def level(number, carry):
        pairs = chunk_pairs(nibble(MASKS, number))
        stacked = jnp.concatenate(
            [jnp.concatenate([state[pair[c]] for pair in pairs], axis=1) for c in range(2)], axis=0
        )
        mixed = product(mats_h[number], mats_l[number], stacked)
        for n, pair in enumerate(pairs):
            for e in range(2):
                block = mixed[e * LANES : (e + 1) * LANES, n * LANES : (n + 1) * LANES]
                real, imag = block[:half], block[half:]
                cosine = cos_ref[pl.ds(number * 8 + pair[e], 1), :]
                sine = sin_ref[pl.ds(number * 8 + pair[e], 1), :]
                state[pair[e], :half, :] = real * cosine - imag * sine
                state[pair[e], half:, :] = real * sine + imag * cosine
        return carry

    def swap(number, carry):
        weight = half >> number
        lane_set = jnp.bitwise_and(iota((LANES, LANES), 1), weight) != 0
        for low, high in chunk_pairs(nibble(MASKS, number)):
            lower, upper = state[low], state[high]
            state[low] = jnp.where(lane_set, pltpu.roll(upper, weight, 1), lower)
            state[high] = jnp.where(lane_set, upper, pltpu.roll(lower, LANES - weight, 1))
        return carry

    def phase(number, done):
        lax.fori_loop(3 * number, jnp.minimum(3 * number + 3, 7), level, 0)
        then = nibble(EXCHANGES_TO, number)
        lax.fori_loop(done, then, swap, 0)
        return then

    lax.fori_loop(0, 3, phase, 0)

    def write(c, carry):
        out_ref[pl.ds(pl.multiple_of(c * LANES, LANES), LANES), :] = state[c].T
        return carry

    lax.fori_loop(0, 8, write, 0)


def transform(sums, prepared):
    box_count, width = sums.shape[0], sums.shape[1] // 2
    return pl.pallas_call(
        levels_kernel,
        out_shape=jax.ShapeDtypeStruct((box_count, width), jnp.float32),
        in_specs=in_vmem(7),
        out_specs=in_vmem(1)[0],
        scratch_shapes=[pltpu.VMEM((8, width, LANES), jnp.float32)],
        compiler_params=params(),
    )(sums, *prepared)


def in_rounds(sources, owner, box, twiddle, prepared):
    box_count, width = twiddle.shape[1], sources.shape[1]

    def body(carry):
        number, sums, _ = carry
        arrived = deliver(pack(number, sources, owner, box, twiddle))
        return (number + 1, *collect(arrived, sums))

    start = (
        jnp.int32(0),
        jnp.zeros((box_count, 2 * width), jnp.float32),
        jnp.ones((1,), jnp.int32),
    )
    _, sums, _ = lax.while_loop(lambda carry: carry[2][0] > 0, body, start)
    return transform(sums, prepared)


def local(sources, owner, box, leaf_op, level_ops, twiddle):
    box_count = twiddle.shape[1]
    packed = pack(jnp.int32(0), sources, owner, box, twiddle)
    arrived = deliver(packed)
    peers = [twiddle] + [swapped(twiddle, "gx", 4 * i) for i in range(1, 4)]
    prepared = prepare(twiddle, leaf_op, level_ops)
    blocks, flag, *tables = finish(arrived, peers, prepared, box_count)
    return lax.cond(
        flag[0] > 0,
        lambda: in_rounds(sources, owner, box, twiddle, [*tables, *prepared[2:]]),
        lambda: blocks,
    )


def solution(mesh):
    in_specs = (
        P(("gx", "gy"), None),
        P(("gx", "gy"), None),
        P(("gx", "gy")),
        P(),
        P(),
        P(None, ("gx", "gy")),
    )
    out_specs = P(("gx", "gy"), None)
    return jax.shard_map(local, mesh=mesh, in_specs=in_specs, out_specs=out_specs, check_vma=False)
```

```python
import jax
import jax.numpy as jnp
from jax import lax
from jax.experimental import pallas as pl
from jax.experimental.pallas import tpu as pltpu
from jax.sharding import PartitionSpec as P

LANES = 128
VMEM_LIMIT = 48 * 1024 * 1024


def swapped(shard, axis, shift):
    return lax.ppermute(shard, axis, [(i, i ^ shift) for i in range(lax.axis_size(axis))])


SLOTS = 40
KEPT = SLOTS - 2
LABEL_ROW = KEPT
FLAG_LANE = KEPT
ANGLE_ROW = KEPT + 1
ANGLE_LANES = (0, 32, 64)
THIRD_ROW = KEPT - 1
SURE = 24
STEP = 4


def bit(value, place):
    return jnp.bitwise_and(jnp.right_shift(value, place), 1)


def bits_to(value, places):
    total = None
    for source, target in places:
        term = jnp.left_shift(bit(value, source), target)
        total = term if total is None else total + term
    return total


def iota(shape, axis):
    return lax.broadcasted_iota(jnp.int32, shape, axis)


def thirds(value):
    high = value.astype(jnp.bfloat16)
    return (high, *split(value - high.astype(jnp.float32)))


def angles_for_all(twiddle_ref, level, lane):
    width = 16 << level
    devices = LANES
    dest = iota((devices, LANES), 0)
    cols = iota((devices, LANES), 1)
    first = bits_to(dest, [(level + 1 + b, 2 - b) for b in range(3)])
    last = range(level + 4, 7)
    group = bits_to(dest, [(b, 6 - b) for b in last])
    rows = jnp.zeros((devices, LANES), jnp.float32)
    for g in range(8):
        part = twiddle_ref[level : level + 1, g * LANES : (g + 1) * LANES]
        rows = jnp.where(first == g, part, rows)
    rows = jnp.where(jnp.right_shift(cols, 4 + level) == group, rows, 0.0)
    fold = jnp.where(cols == lane + jnp.bitwise_and(dest, width - 1), 1.0, 0.0)
    fold = fold.astype(jnp.bfloat16)
    return sum(jnp.dot(part, fold, preferred_element_type=jnp.float32) for part in thirds(rows))


def pack_kernel(
    round_ref, dev_ref, owner_hbm, box_hbm, twiddle_hbm, src_hbm, out_ref,
    owner_ref, box_ref, twiddle_ref, src_ref, slot_vmem, slot_smem, hits, parts, sems,
):
    pairs = (
        (owner_hbm, owner_ref), (box_hbm, box_ref), (twiddle_hbm, twiddle_ref), (src_hbm, src_ref),
        (slot_vmem, slot_smem),
    )
    copies = [pltpu.make_async_copy(a, b, sems.at[n]) for n, (a, b) in enumerate(pairs)]
    for copy in copies[:4]:
        copy.start()

    def clear(n, carry):
        out_ref[pl.ds(pl.multiple_of(n * 64, 64), 64), :] = jnp.zeros((64, LANES), jnp.float32)
        return carry

    lax.fori_loop(0, out_ref.shape[0] // 64, clear, 0)
    copies[0].wait()
    copies[1].wait()
    chunks = owner_ref.shape[0]
    devices = LANES
    number, device = round_ref[0], dev_ref[0]

    def kept(dest):
        shared = jnp.bitwise_and(jnp.bitwise_xor(dest, device), 15) == 0
        return jnp.where(shared, THIRD_ROW, KEPT)

    rows = iota((devices, LANES), 0)
    cols = iota((devices, LANES), 1)
    upto = jnp.where(rows <= cols, 1.0, 0.0).astype(jnp.bfloat16)
    high_half = rows < 64
    rank_of_row = jnp.bitwise_and(rows, 63)
    owner = owner_ref[...]
    box = box_ref[...]
    dest = bits_to(box, [(3 + b, 6 - b) for b in range(7)])
    places = [(0, 9), (1, 8), (2, 7), (4, 6), (5, 5), (3, 4), (6, 3)]
    target = bits_to(owner, places) + jnp.bitwise_and(box, 7) + 1
    target_high = jnp.right_shift(target, 5)
    target_low = jnp.bitwise_and(target, 31)
    count = jnp.zeros((devices, 1), jnp.float32)
    for c in range(chunks):
        dest_c = dest[c : c + 1, :]
        hit = dest_c == rows
        onehot = jnp.where(hit, 1.0, 0.0).astype(jnp.bfloat16)
        upto_here = jnp.dot(onehot, upto, preferred_element_type=jnp.float32) + count
        rank = jnp.sum(jnp.where(hit, upto_here, 0.0), axis=0, keepdims=True) - 1.0
        count = upto_here[:, LANES - 1 : LANES]
        kept_c = kept(dest_c)
        rank = rank.astype(jnp.int32) - number * kept_c
        now = jnp.logical_and(rank >= 0, rank < kept_c)
        slot_vmem[c : c + 1, :] = dest_c * SLOTS + jnp.where(now, rank, LABEL_ROW)
        part = jnp.where(high_half, target_high[c : c + 1, :], target_low[c : c + 1, :])
        part = jnp.where(rank == rank_of_row, part, 0).astype(jnp.float32).astype(jnp.bfloat16)
        hits[:, c * LANES : (c + 1) * LANES] = onehot
        parts[:, c * LANES : (c + 1) * LANES] = part
    copies[4].start()
    labels = lax.dot_general(
        hits[...], parts[...], (((1,), (1,)), ((), ())), preferred_element_type=jnp.float32
    )
    copies[2].wait()
    angle_rows = sum(angles_for_all(twiddle_ref, n, lane) for n, lane in enumerate(ANGLE_LANES))
    passes = kept(rows)
    most = jnp.max(count - ((number + 1) * passes[:, :1]).astype(jnp.float32), axis=0, keepdims=True)
    left = jnp.where(most > 0.0, 1.0, 0.0)
    label_rows = labels * 32.0 + pltpu.roll(labels, 64, 1)
    label_rows = jnp.where(cols < passes, label_rows, jnp.where(cols == FLAG_LANE, left, 0.0))
    copies[4].wait()
    copies[3].wait()

    def move(c, carry):
        base = pl.multiple_of(c * LANES, LANES)
        for k in range(LANES):
            out_ref[pl.ds(slot_smem[c, k], 1), :] = src_ref[pl.ds(base + k, 1), :]
        return carry

    lax.fori_loop(0, chunks, move, 0)
    out_ref[pl.ds(LABEL_ROW, devices, stride=SLOTS), :] = label_rows
    out_ref[pl.ds(ANGLE_ROW, devices, stride=SLOTS), :] = angle_rows
    for h in range(8):
        part = 4 * (h & 1) + (h & 2) + (h >> 2)
        out_ref[pl.ds(third_place(device, h), 1), :] = twiddle_ref[
            3:4, part * LANES : (part + 1) * LANES
        ]


def third_place(device, h):
    return ((device & 15) + 16 * h) * SLOTS + THIRD_ROW


def params():
    return pltpu.CompilerParams(vmem_limit_bytes=VMEM_LIMIT)


def in_vmem(count):
    return [pl.BlockSpec(memory_space=pltpu.VMEM)] * count


def anywhere(count):
    return [pl.BlockSpec(memory_space=pl.ANY)] * count


def in_smem():
    return [pl.BlockSpec(memory_space=pltpu.SMEM)]


def pack(number, sources, owner, box, twiddle):
    count, width = sources.shape
    chunks = count // LANES
    block = pltpu.VMEM((chunks, LANES), jnp.int32)
    return pl.pallas_call(
        pack_kernel,
        out_shape=jax.ShapeDtypeStruct((LANES * SLOTS, width), jnp.float32),
        in_specs=in_smem() * 2 + anywhere(4),
        out_specs=in_vmem(1)[0],
        scratch_shapes=[
            block,
            block,
            pltpu.VMEM(twiddle.shape, jnp.float32),
            pltpu.VMEM(sources.shape, jnp.float32),
            block,
            pltpu.SMEM((chunks, LANES), jnp.int32),
            pltpu.VMEM((LANES, count), jnp.bfloat16),
            pltpu.VMEM((LANES, count), jnp.bfloat16),
            pltpu.SemaphoreType.DMA((5,)),
        ],
        compiler_params=params(),
    )(
        number.reshape(1),
        own_number(),
        owner.reshape(chunks, LANES),
        box.reshape(chunks, LANES),
        twiddle,
        sources,
    )


def deliver(packed):
    width = packed.shape[1]
    return lax.all_to_all(
        packed.reshape(-1, SLOTS, width), ("gx", "gy"), split_axis=0, concat_axis=0, tiled=True
    ).reshape(-1, width)


LAYOUTS = (
    ("e0", "D1", "D2", "D4", "D5", "D3", "D6"),
    ("e0", "e1", "D2", "D4", "D5", "D3", "D6"),
    ("e0", "e1", "e2", "D4", "D5", "D3", "D6"),
    ("D4", "D5", "e3", "e0", "e1", "e2", "D6"),
    ("e4", "D5", "e3", "e0", "e1", "e2", "D6"),
    ("e4", "e5", "e3", "e0", "e1", "e2", "D6"),
    ("e4", "e5", "e6", "e0", "e1", "e2", "e3"),
)
MASKS = 0x1241124
EXCHANGES_TO = 0x743


def twiddle_place(level, position, device):
    names = {}
    for place, name in enumerate(LAYOUTS[level]):
        names[name] = bit(position, 9 - place)
    for b in range(3):
        names["q" + str(b)] = bit(position, b)
    owner = 0
    for b in range(7):
        here = names["D" + str(b)] if b > level else bit(device, b)
        owner = owner + jnp.left_shift(here, b)
    order = [bit(device, b) for b in range(level + 1, 7)]
    order = order + [names["q2"], names["q1"], names["q0"]]
    order = order + [names["e" + str(b)] for b in range(level + 1)]
    index = 0
    for value in order:
        index = index * 2 + value
    return owner, index


def picked(held, row, column):
    pick = jnp.where(row == iota((held.shape[0], 8 * LANES), 0), 1.0, 0.0).astype(jnp.bfloat16)
    spread = sum(
        lax.dot_general(part, pick, (((0,), (0,)), ((), ())), preferred_element_type=jnp.float32)
        for part in thirds(held)
    )
    mine = column == iota((LANES, 8 * LANES), 0)
    angle = jnp.sum(jnp.where(mine, spread, 0.0), axis=0, keepdims=True)
    return jnp.concatenate([angle[:, c * LANES : (c + 1) * LANES] for c in range(8)], axis=0)


def split(value):
    high = value.astype(jnp.bfloat16)
    low = (value - high.astype(jnp.float32)).astype(jnp.bfloat16)
    return high, low


def prepare_kernel(
    dev_ref, twiddle_ref, leaf_ref, ops_ref, cos_ref, sin_ref, leaf_h, leaf_l, mats_h, mats_l
):
    cos_ref[0:48, :] = jnp.zeros((48, LANES), jnp.float32)
    sin_ref[0:48, :] = jnp.zeros((48, LANES), jnp.float32)
    _, index = twiddle_place(6, iota((1, 8 * LANES), 1), dev_ref[0])
    angles = [twiddle_ref[6:7, c * LANES : (c + 1) * LANES] for c in range(8)]
    row, column = jnp.right_shift(index, 7), jnp.bitwise_and(index, LANES - 1)
    angle = picked(jnp.concatenate(angles, axis=0), row, column)
    cos_ref[48:56, :] = jnp.cos(angle)
    sin_ref[48:56, :] = jnp.sin(angle)

    def block(real, imag):
        top = jnp.concatenate([real, imag], axis=1)
        bottom = jnp.concatenate([-imag, real], axis=1)
        return jnp.concatenate([top, bottom], axis=0).T

    leaf = block(leaf_ref[0], leaf_ref[1])
    leaf_h[...], leaf_l[...] = split(leaf)

    def build(n, carry):
        level, e, c = n // 4, lax.rem(n, 4) // 2, lax.rem(n, 2)
        high, low = split(block(ops_ref[level, e, c, 0], ops_ref[level, e, c, 1]))
        out = pl.ds(pl.multiple_of(e * LANES, LANES), LANES)
        across = pl.ds(pl.multiple_of(c * LANES, LANES), LANES)
        mats_h[level, out, across] = high
        mats_l[level, out, across] = low
        return carry

    lax.fori_loop(0, 4 * ops_ref.shape[0], build, 0, unroll=2)


def prepare(twiddle, leaf_op, level_ops):
    levels, count = twiddle.shape
    width = 2 * leaf_op.shape[1]
    return pl.pallas_call(
        prepare_kernel,
        out_shape=[
            jax.ShapeDtypeStruct((levels * count // LANES, LANES), jnp.float32),
            jax.ShapeDtypeStruct((levels * count // LANES, LANES), jnp.float32),
            jax.ShapeDtypeStruct((width, width), jnp.bfloat16),
            jax.ShapeDtypeStruct((width, width), jnp.bfloat16),
            jax.ShapeDtypeStruct((levels, 2 * width, 2 * width), jnp.bfloat16),
            jax.ShapeDtypeStruct((levels, 2 * width, 2 * width), jnp.bfloat16),
        ],
        in_specs=in_smem() + in_vmem(3),
        out_specs=in_vmem(6),
        compiler_params=params(),
    )(own_number(), twiddle, leaf_op, level_ops)


def own_number():
    device = lax.axis_index("gx") * lax.axis_size("gy") + lax.axis_index("gy")
    return device.reshape(1).astype(jnp.int32)


def product(high, low, value):
    value_high, value_low = split(value)
    total = jnp.dot(high, value_high, preferred_element_type=jnp.float32)
    total += jnp.dot(high, value_low, preferred_element_type=jnp.float32)
    total += jnp.dot(low, value_high, preferred_element_type=jnp.float32)
    return total


def moved_rotations(angles, third, peers, device, cos_ref, sin_ref):
    position = iota((1, 8 * LANES), 1)
    angle = []
    for level in range(6):
        owner, index = twiddle_place(level, position, device)
        if level < 3:
            held, row = angles, owner
            column = ANGLE_LANES[level] + jnp.bitwise_and(index, (16 << level) - 1)
        elif level == 3:
            held, row = third, jnp.right_shift(owner, 4)
            column = jnp.bitwise_and(index, LANES - 1)
        else:
            taken = 2 ** (level - 3)
            fixed = 0
            for b in range(level + 1, 7):
                fixed = fixed * 2 + bit(device, b)
            parts = []
            for k in range(taken):
                lane = pl.multiple_of((fixed * taken + k) * LANES, LANES)
                parts += [peer[level : level + 1, pl.ds(lane, LANES)] for peer in peers]
            held = jnp.concatenate(parts, axis=0)
            row = jnp.right_shift(jnp.bitwise_xor(owner, device), 5)
            row = row + 4 * jnp.bitwise_and(jnp.right_shift(index, 7), taken - 1)
            column = jnp.bitwise_and(index, LANES - 1)
        angle.append(picked(held, row, column))
    angle = jnp.concatenate(angle, axis=0)
    cos_ref[0:48, :] = jnp.cos(angle)
    sin_ref[0:48, :] = jnp.sin(angle)


def third_angles(x_ref, device):
    rows = [x_ref[pl.ds(third_place(device, h), 1), :] for h in range(8)]
    return jnp.concatenate(rows, axis=0)


def add_rows(x_ref, names, first, count):
    ranks = [first + k for k in range(count)]
    value = jnp.concatenate([x_ref[pl.ds(r, LANES, stride=SLOTS), :] for r in ranks], axis=0)
    name = jnp.concatenate([names[pl.ds(r, 1), :] for r in ranks], axis=1)
    targets = iota((8 * LANES, count * LANES), 0).astype(jnp.float32)
    pick = jnp.where(targets == name, 1.0, 0.0).astype(jnp.bfloat16)
    both = jnp.concatenate(split(value), axis=1)
    return jnp.dot(pick, both, preferred_element_type=jnp.float32)


def chunk_pairs(mask):
    lows = [2 * n - (n & (mask - 1)) for n in range(4)]
    return [(low, low + mask) for low in lows]


def nibble(table, n):
    return (table >> (4 * n)) & 15


def exchange(state, mask, weight):
    lane_set = jnp.bitwise_and(iota((LANES, LANES), 1), weight) != 0
    out = list(state)
    for low, high in chunk_pairs(mask):
        lower, upper = state[low], state[high]
        out[low] = jnp.where(lane_set, pltpu.roll(upper, weight, 1), lower)
        out[high] = jnp.where(lane_set, upper, pltpu.roll(lower, LANES - weight, 1))
    return out


def butterfly(state, mask, high, low, cos_ref, sin_ref, number):
    half = LANES // 2
    stacked = jnp.concatenate(
        [jnp.concatenate([state[pair[c]] for pair in chunk_pairs(mask)], axis=1) for c in range(2)],
        axis=0,
    )
    mixed = product(high, low, stacked)
    out = list(state)
    for n, pair in enumerate(chunk_pairs(mask)):
        for e in range(2):
            block = mixed[e * LANES : (e + 1) * LANES, n * LANES : (n + 1) * LANES]
            real, imag = block[:half], block[half:]
            place = number * 8 + pair[e]
            cosine = cos_ref[place : place + 1, :]
            sine = sin_ref[place : place + 1, :]
            out[pair[e]] = jnp.concatenate(
                [real * cosine - imag * sine, real * sine + imag * cosine], axis=0
            )
    return out


def finish_kernel(
    dev_ref, x_ref, peer0, peer1, peer2, peer3,
    cos_in, sin_in, leaf_h_in, leaf_l_in, mats_h_in, mats_l_in,
    out_ref, flag_ref, cos_ref, sin_ref,
    sums, names, cos_far, sin_far, leaf_h, leaf_l, mats_h, mats_l, sems,
):
    pairs = (
        (cos_in, cos_far), (sin_in, sin_far), (leaf_h_in, leaf_h), (leaf_l_in, leaf_l),
        (mats_h_in, mats_h), (mats_l_in, mats_l),
    )
    copies = [pltpu.make_async_copy(a, b, sems.at[n]) for n, (a, b) in enumerate(pairs)]
    for copy in copies:
        copy.start()
    labels = x_ref[pl.ds(LABEL_ROW, LANES, stride=SLOTS), :]
    names[...] = labels.T - 1.0
    flag_ref[0] = jnp.max(names[FLAG_LANE : FLAG_LANE + 1, :] + 1.0).astype(jnp.int32)
    column = iota((LANES, LANES), 1)
    filled = jnp.logical_and(labels > 0.0, column < KEPT)
    most = jnp.max(jnp.where(filled, column + 1, 0).astype(jnp.float32)).astype(jnp.int32)
    sums[...] = add_rows(x_ref, names, 0, SURE)
    angles = x_ref[pl.ds(ANGLE_ROW, LANES, stride=SLOTS), :]
    third = third_angles(x_ref, dev_ref[0])
    peers = (peer0, peer1, peer2, peer3)
    moved_rotations(angles, third, peers, dev_ref[0], cos_ref, sin_ref)
    for first in range(SURE, SLOTS, STEP):

        @pl.when(most > first)
        def _():
            sums[...] += add_rows(x_ref, names, first, STEP)

    for copy in copies:
        copy.wait()
    cos_ref[48:, :] = cos_far[48:, :]
    sin_ref[48:, :] = sin_far[48:, :]
    state = []
    for c in range(8):
        block = sums[c * LANES : (c + 1) * LANES, :]
        state.append((block[:, :LANES] + block[:, LANES:]).T)
    leafed = product(leaf_h[...], leaf_l[...], jnp.concatenate(state, axis=1))
    state = [leafed[:, c * LANES : (c + 1) * LANES] for c in range(8)]
    done = 0
    for number in range(7):
        mask = nibble(MASKS, number)
        state = butterfly(state, mask, mats_h[number], mats_l[number], cos_ref, sin_ref, number)
        if number in (2, 5, 6):
            then = nibble(EXCHANGES_TO, number // 3)
            for n in range(done, then):
                state = exchange(state, nibble(MASKS, n), LANES // 2 >> n)
            done = then
    for c in range(8):
        out_ref[c * LANES : (c + 1) * LANES, :] = state[c].T


def finish(arrived, peers, prepared, box_count):
    width = arrived.shape[1]
    table = jax.ShapeDtypeStruct(prepared[0].shape, jnp.float32)
    return pl.pallas_call(
        finish_kernel,
        out_shape=[
            jax.ShapeDtypeStruct((box_count, width), jnp.float32),
            jax.ShapeDtypeStruct((1,), jnp.int32),
            table,
            table,
        ],
        in_specs=in_smem() + in_vmem(5) + anywhere(6),
        out_specs=in_vmem(1) + in_smem() + in_vmem(2),
        scratch_shapes=[
            pltpu.VMEM((box_count, 2 * width), jnp.float32),
            pltpu.VMEM((LANES, LANES), jnp.float32),
        ]
        + [pltpu.VMEM(array.shape, array.dtype) for array in prepared]
        + [pltpu.SemaphoreType.DMA((len(prepared),))],
        compiler_params=params(),
    )(own_number(), arrived, *peers, *prepared)


def collect_kernel(x_ref, before_ref, sums, flag_ref, names):
    labels = x_ref[pl.ds(LABEL_ROW, LANES, stride=SLOTS), :]
    names[...] = labels.T - 1.0
    flag_ref[0] = jnp.max(names[FLAG_LANE : FLAG_LANE + 1, :] + 1.0).astype(jnp.int32)
    names[FLAG_LANE : FLAG_LANE + 1, :] = jnp.full((1, LANES), -1.0)
    sums[...] = before_ref[...]

    def body(pair, carry):
        sums[...] += add_rows(x_ref, names, 2 * pair, 2)
        return carry

    lax.fori_loop(0, SLOTS // 2, body, 0)


def collect(arrived, sums):
    return pl.pallas_call(
        collect_kernel,
        out_shape=[
            jax.ShapeDtypeStruct(sums.shape, jnp.float32),
            jax.ShapeDtypeStruct((1,), jnp.int32),
        ],
        in_specs=in_vmem(2),
        out_specs=in_vmem(1) + in_smem(),
        scratch_shapes=[pltpu.VMEM((LANES, LANES), jnp.float32)],
        compiler_params=params(),
    )(arrived, sums)


def levels_kernel(sums, cos_ref, sin_ref, leaf_h, leaf_l, mats_h, mats_l, out_ref, state):
    half = LANES // 2

    def leaf(c, carry):
        block = sums[pl.ds(pl.multiple_of(c * LANES, LANES), LANES), :]
        state[c] = product(leaf_h[...], leaf_l[...], (block[:, :LANES] + block[:, LANES:]).T)
        return carry

    lax.fori_loop(0, 8, leaf, 0)

    def level(number, carry):
        pairs = chunk_pairs(nibble(MASKS, number))
        stacked = jnp.concatenate(
            [jnp.concatenate([state[pair[c]] for pair in pairs], axis=1) for c in range(2)], axis=0
        )
        mixed = product(mats_h[number], mats_l[number], stacked)
        for n, pair in enumerate(pairs):
            for e in range(2):
                block = mixed[e * LANES : (e + 1) * LANES, n * LANES : (n + 1) * LANES]
                real, imag = block[:half], block[half:]
                cosine = cos_ref[pl.ds(number * 8 + pair[e], 1), :]
                sine = sin_ref[pl.ds(number * 8 + pair[e], 1), :]
                state[pair[e], :half, :] = real * cosine - imag * sine
                state[pair[e], half:, :] = real * sine + imag * cosine
        return carry

    def swap(number, carry):
        weight = half >> number
        lane_set = jnp.bitwise_and(iota((LANES, LANES), 1), weight) != 0
        for low, high in chunk_pairs(nibble(MASKS, number)):
            lower, upper = state[low], state[high]
            state[low] = jnp.where(lane_set, pltpu.roll(upper, weight, 1), lower)
            state[high] = jnp.where(lane_set, upper, pltpu.roll(lower, LANES - weight, 1))
        return carry

    def phase(number, done):
        lax.fori_loop(3 * number, jnp.minimum(3 * number + 3, 7), level, 0)
        then = nibble(EXCHANGES_TO, number)
        lax.fori_loop(done, then, swap, 0)
        return then

    lax.fori_loop(0, 3, phase, 0)

    def write(c, carry):
        out_ref[pl.ds(pl.multiple_of(c * LANES, LANES), LANES), :] = state[c].T
        return carry

    lax.fori_loop(0, 8, write, 0)


def transform(sums, prepared):
    box_count, width = sums.shape[0], sums.shape[1] // 2
    return pl.pallas_call(
        levels_kernel,
        out_shape=jax.ShapeDtypeStruct((box_count, width), jnp.float32),
        in_specs=in_vmem(7),
        out_specs=in_vmem(1)[0],
        scratch_shapes=[pltpu.VMEM((8, width, LANES), jnp.float32)],
        compiler_params=params(),
    )(sums, *prepared)


def in_rounds(sources, owner, box, twiddle, prepared):
    box_count, width = twiddle.shape[1], sources.shape[1]

    def body(carry):
        number, sums, _ = carry
        arrived = deliver(pack(number, sources, owner, box, twiddle))
        return (number + 1, *collect(arrived, sums))

    start = (
        jnp.int32(0),
        jnp.zeros((box_count, 2 * width), jnp.float32),
        jnp.ones((1,), jnp.int32),
    )
    _, sums, _ = lax.while_loop(lambda carry: carry[2][0] > 0, body, start)
    return transform(sums, prepared)


def local(sources, owner, box, leaf_op, level_ops, twiddle):
    box_count = twiddle.shape[1]
    packed = pack(jnp.int32(0), sources, owner, box, twiddle)
    arrived = deliver(packed)
    peers = [twiddle] + [swapped(twiddle, "gx", 4 * i) for i in range(1, 4)]
    prepared = prepare(twiddle, leaf_op, level_ops)
    blocks, flag, *tables = finish(arrived, peers, prepared, box_count)
    return lax.cond(
        flag[0] > 0,
        lambda: in_rounds(sources, owner, box, twiddle, [*tables, *prepared[2:]]),
        lambda: blocks,
    )


def solution(mesh):
    in_specs = (
        P(("gx", "gy"), None),
        P(("gx", "gy"), None),
        P(("gx", "gy")),
        P(),
        P(),
        P(None, ("gx", "gy")),
    )
    out_specs = P(("gx", "gy"), None)
    return jax.shard_map(local, mesh=mesh, in_specs=in_specs, out_specs=out_specs, check_vma=False)
```

```python
import jax
import jax.numpy as jnp
from jax import lax
from jax.experimental import pallas as pl
from jax.experimental.pallas import tpu as pltpu
from jax.sharding import PartitionSpec as P

LANES = 128
VMEM_LIMIT = 48 * 1024 * 1024


def swapped(shard, axis, shift):
    return lax.ppermute(shard, axis, [(i, i ^ shift) for i in range(lax.axis_size(axis))])


SLOTS = 40
KEPT = SLOTS - 2
LABEL_ROW = KEPT
FLAG_LANE = KEPT
ANGLE_ROW = KEPT + 1
ANGLE_LANES = (0, 32, 64)
THIRD_ROW = KEPT - 1
SURE = 24
STEP = 4


def bit(value, place):
    return jnp.bitwise_and(jnp.right_shift(value, place), 1)


def bits_to(value, places):
    total = None
    for source, target in places:
        term = jnp.left_shift(bit(value, source), target)
        total = term if total is None else total + term
    return total


def iota(shape, axis):
    return lax.broadcasted_iota(jnp.int32, shape, axis)


def thirds(value):
    high = value.astype(jnp.bfloat16)
    return (high, *split(value - high.astype(jnp.float32)))


def angles_for_all(twiddle_ref, level, lane):
    width = 16 << level
    devices = LANES
    dest = iota((devices, LANES), 0)
    cols = iota((devices, LANES), 1)
    first = bits_to(dest, [(level + 1 + b, 2 - b) for b in range(3)])
    last = range(level + 4, 7)
    group = bits_to(dest, [(b, 6 - b) for b in last])
    rows = jnp.zeros((devices, LANES), jnp.float32)
    for g in range(8):
        part = twiddle_ref[level : level + 1, g * LANES : (g + 1) * LANES]
        rows = jnp.where(first == g, part, rows)
    rows = jnp.where(jnp.right_shift(cols, 4 + level) == group, rows, 0.0)
    fold = jnp.where(cols == lane + jnp.bitwise_and(dest, width - 1), 1.0, 0.0)
    fold = fold.astype(jnp.bfloat16)
    return sum(jnp.dot(part, fold, preferred_element_type=jnp.float32) for part in thirds(rows))


def pack_kernel(
    round_ref, dev_ref, owner_hbm, box_hbm, twiddle_hbm, src_hbm, out_ref,
    owner_ref, box_ref, twiddle_ref, src_ref, slot_vmem, slot_smem, hits, parts, sems,
):
    pairs = (
        (owner_hbm, owner_ref), (box_hbm, box_ref), (twiddle_hbm, twiddle_ref), (src_hbm, src_ref),
        (slot_vmem, slot_smem),
    )
    copies = [pltpu.make_async_copy(a, b, sems.at[n]) for n, (a, b) in enumerate(pairs)]
    for copy in copies[:4]:
        copy.start()

    def clear(n, carry):
        out_ref[pl.ds(pl.multiple_of(n * 64, 64), 64), :] = jnp.zeros((64, LANES), jnp.float32)
        return carry

    lax.fori_loop(0, out_ref.shape[0] // 64, clear, 0)
    copies[0].wait()
    copies[1].wait()
    chunks = owner_ref.shape[0]
    devices = LANES
    number, device = round_ref[0], dev_ref[0]

    def kept(dest):
        shared = jnp.bitwise_and(jnp.bitwise_xor(dest, device), 15) == 0
        return jnp.where(shared, THIRD_ROW, KEPT)

    rows = iota((devices, LANES), 0)
    cols = iota((devices, LANES), 1)
    upto = jnp.where(rows <= cols, 1.0, 0.0).astype(jnp.bfloat16)
    high_half = rows < 64
    rank_of_row = jnp.bitwise_and(rows, 63)
    owner = owner_ref[...]
    box = box_ref[...]
    dest = bits_to(box, [(3 + b, 6 - b) for b in range(7)])
    places = [(0, 9), (1, 8), (2, 7), (4, 6), (5, 5), (3, 4), (6, 3)]
    target = bits_to(owner, places) + jnp.bitwise_and(box, 7) + 1
    target_high = jnp.right_shift(target, 5)
    target_low = jnp.bitwise_and(target, 31)
    count = jnp.zeros((devices, 1), jnp.float32)
    for c in range(chunks):
        dest_c = dest[c : c + 1, :]
        hit = dest_c == rows
        onehot = jnp.where(hit, 1.0, 0.0).astype(jnp.bfloat16)
        upto_here = jnp.dot(onehot, upto, preferred_element_type=jnp.float32) + count
        rank = jnp.sum(jnp.where(hit, upto_here, 0.0), axis=0, keepdims=True) - 1.0
        count = upto_here[:, LANES - 1 : LANES]
        kept_c = kept(dest_c)
        rank = rank.astype(jnp.int32) - number * kept_c
        now = jnp.logical_and(rank >= 0, rank < kept_c)
        slot_vmem[c : c + 1, :] = dest_c * SLOTS + jnp.where(now, rank, LABEL_ROW)
        part = jnp.where(high_half, target_high[c : c + 1, :], target_low[c : c + 1, :])
        part = jnp.where(rank == rank_of_row, part, 0).astype(jnp.float32).astype(jnp.bfloat16)
        hits[:, c * LANES : (c + 1) * LANES] = onehot
        parts[:, c * LANES : (c + 1) * LANES] = part
    copies[4].start()
    labels = lax.dot_general(
        hits[...], parts[...], (((1,), (1,)), ((), ())), preferred_element_type=jnp.float32
    )
    copies[2].wait()
    angle_rows = sum(angles_for_all(twiddle_ref, n, lane) for n, lane in enumerate(ANGLE_LANES))
    passes = kept(rows)
    most = jnp.max(count - ((number + 1) * passes[:, :1]).astype(jnp.float32), axis=0, keepdims=True)
    left = jnp.where(most > 0.0, 1.0, 0.0)
    label_rows = labels * 32.0 + pltpu.roll(labels, 64, 1)
    label_rows = jnp.where(cols < passes, label_rows, jnp.where(cols == FLAG_LANE, left, 0.0))
    copies[4].wait()
    copies[3].wait()

    def move(c, carry):
        base = pl.multiple_of(c * LANES, LANES)
        for k in range(LANES):
            out_ref[pl.ds(slot_smem[c, k], 1), :] = src_ref[pl.ds(base + k, 1), :]
        return carry

    lax.fori_loop(0, chunks, move, 0)
    out_ref[pl.ds(LABEL_ROW, devices, stride=SLOTS), :] = label_rows
    out_ref[pl.ds(ANGLE_ROW, devices, stride=SLOTS), :] = angle_rows
    for h in range(8):
        part = 4 * (h & 1) + (h & 2) + (h >> 2)
        out_ref[pl.ds(third_place(device, h), 1), :] = twiddle_ref[
            3:4, part * LANES : (part + 1) * LANES
        ]


def third_place(device, h):
    return ((device & 15) + 16 * h) * SLOTS + THIRD_ROW


def params():
    return pltpu.CompilerParams(vmem_limit_bytes=VMEM_LIMIT)


def in_vmem(count):
    return [pl.BlockSpec(memory_space=pltpu.VMEM)] * count


def anywhere(count):
    return [pl.BlockSpec(memory_space=pl.ANY)] * count


def in_smem():
    return [pl.BlockSpec(memory_space=pltpu.SMEM)]


def pack(number, sources, owner, box, twiddle):
    count, width = sources.shape
    chunks = count // LANES
    block = pltpu.VMEM((chunks, LANES), jnp.int32)
    return pl.pallas_call(
        pack_kernel,
        out_shape=jax.ShapeDtypeStruct((LANES * SLOTS, width), jnp.float32),
        in_specs=in_smem() * 2 + anywhere(4),
        out_specs=in_vmem(1)[0],
        scratch_shapes=[
            block,
            block,
            pltpu.VMEM(twiddle.shape, jnp.float32),
            pltpu.VMEM(sources.shape, jnp.float32),
            block,
            pltpu.SMEM((chunks, LANES), jnp.int32),
            pltpu.VMEM((LANES, count), jnp.bfloat16),
            pltpu.VMEM((LANES, count), jnp.bfloat16),
            pltpu.SemaphoreType.DMA((5,)),
        ],
        compiler_params=params(),
    )(
        number.reshape(1),
        own_number(),
        owner.reshape(chunks, LANES),
        box.reshape(chunks, LANES),
        twiddle,
        sources,
    )


def deliver(packed):
    width = packed.shape[1]
    return lax.all_to_all(
        packed.reshape(-1, SLOTS, width), ("gx", "gy"), split_axis=0, concat_axis=0, tiled=True
    ).reshape(-1, width)


LAYOUTS = (
    ("e0", "D1", "D2", "D4", "D5", "D3", "D6"),
    ("e0", "e1", "D2", "D4", "D5", "D3", "D6"),
    ("e0", "e1", "e2", "D4", "D5", "D3", "D6"),
    ("D4", "D5", "e3", "e0", "e1", "e2", "D6"),
    ("e4", "D5", "e3", "e0", "e1", "e2", "D6"),
    ("e4", "e5", "e3", "e0", "e1", "e2", "D6"),
    ("e4", "e5", "e6", "e0", "e1", "e2", "e3"),
)
MASKS = 0x1241124
EXCHANGES_TO = 0x743


def twiddle_place(level, position, device):
    names = {}
    for place, name in enumerate(LAYOUTS[level]):
        names[name] = bit(position, 9 - place)
    for b in range(3):
        names["q" + str(b)] = bit(position, b)
    owner = 0
    for b in range(7):
        here = names["D" + str(b)] if b > level else bit(device, b)
        owner = owner + jnp.left_shift(here, b)
    order = [bit(device, b) for b in range(level + 1, 7)]
    order = order + [names["q2"], names["q1"], names["q0"]]
    order = order + [names["e" + str(b)] for b in range(level + 1)]
    index = 0
    for value in order:
        index = index * 2 + value
    return owner, index


def picked(held, row, column):
    pick = jnp.where(row == iota((held.shape[0], 8 * LANES), 0), 1.0, 0.0).astype(jnp.bfloat16)
    spread = sum(
        lax.dot_general(part, pick, (((0,), (0,)), ((), ())), preferred_element_type=jnp.float32)
        for part in thirds(held)
    )
    mine = column == iota((LANES, 8 * LANES), 0)
    angle = jnp.sum(jnp.where(mine, spread, 0.0), axis=0, keepdims=True)
    return jnp.concatenate([angle[:, c * LANES : (c + 1) * LANES] for c in range(8)], axis=0)


def split(value):
    high = value.astype(jnp.bfloat16)
    low = (value - high.astype(jnp.float32)).astype(jnp.bfloat16)
    return high, low


def prepare_kernel(
    dev_ref, twiddle_ref, leaf_ref, ops_ref, cos_ref, sin_ref, mats_h, mats_l
):
    cos_ref[0:48, :] = jnp.zeros((48, LANES), jnp.float32)
    sin_ref[0:48, :] = jnp.zeros((48, LANES), jnp.float32)
    _, index = twiddle_place(6, iota((1, 8 * LANES), 1), dev_ref[0])
    angles = [twiddle_ref[6:7, c * LANES : (c + 1) * LANES] for c in range(8)]
    row, column = jnp.right_shift(index, 7), jnp.bitwise_and(index, LANES - 1)
    angle = picked(jnp.concatenate(angles, axis=0), row, column)
    cos_ref[48:56, :] = jnp.cos(angle)
    sin_ref[48:56, :] = jnp.sin(angle)

    def block(real, imag):
        top = jnp.concatenate([real, imag], axis=1)
        bottom = jnp.concatenate([-imag, real], axis=1)
        return jnp.concatenate([top, bottom], axis=0).T

    leaf = block(leaf_ref[0], leaf_ref[1])

    def build(n, carry):
        level, e, c = n // 4, lax.rem(n, 4) // 2, lax.rem(n, 2)
        matrix = block(ops_ref[level, e, c, 0], ops_ref[level, e, c, 1])
        led = jnp.dot(
            matrix, leaf, precision=lax.Precision.HIGHEST, preferred_element_type=jnp.float32
        )
        high, low = split(jnp.where(level == 0, led, matrix))
        out = pl.ds(pl.multiple_of(e * LANES, LANES), LANES)
        across = pl.ds(pl.multiple_of(c * LANES, LANES), LANES)
        mats_h[level, out, across] = high
        mats_l[level, out, across] = low
        return carry

    lax.fori_loop(0, 4 * ops_ref.shape[0], build, 0, unroll=2)


def prepare(twiddle, leaf_op, level_ops):
    levels, count = twiddle.shape
    width = 2 * leaf_op.shape[1]
    return pl.pallas_call(
        prepare_kernel,
        out_shape=[
            jax.ShapeDtypeStruct((levels * count // LANES, LANES), jnp.float32),
            jax.ShapeDtypeStruct((levels * count // LANES, LANES), jnp.float32),
            jax.ShapeDtypeStruct((levels, 2 * width, 2 * width), jnp.bfloat16),
            jax.ShapeDtypeStruct((levels, 2 * width, 2 * width), jnp.bfloat16),
        ],
        in_specs=in_smem() + in_vmem(3),
        out_specs=in_vmem(4),
        compiler_params=params(),
    )(own_number(), twiddle, leaf_op, level_ops)


def own_number():
    device = lax.axis_index("gx") * lax.axis_size("gy") + lax.axis_index("gy")
    return device.reshape(1).astype(jnp.int32)


def product(high, low, value):
    value_high, value_low = split(value)
    total = jnp.dot(high, value_high, preferred_element_type=jnp.float32)
    total += jnp.dot(high, value_low, preferred_element_type=jnp.float32)
    total += jnp.dot(low, value_high, preferred_element_type=jnp.float32)
    return total


def moved_rotations(angles, third, peers, device, cos_ref, sin_ref):
    position = iota((1, 8 * LANES), 1)
    angle = []
    for level in range(6):
        owner, index = twiddle_place(level, position, device)
        if level < 3:
            held, row = angles, owner
            column = ANGLE_LANES[level] + jnp.bitwise_and(index, (16 << level) - 1)
        elif level == 3:
            held, row = third, jnp.right_shift(owner, 4)
            column = jnp.bitwise_and(index, LANES - 1)
        else:
            taken = 2 ** (level - 3)
            fixed = 0
            for b in range(level + 1, 7):
                fixed = fixed * 2 + bit(device, b)
            parts = []
            for k in range(taken):
                lane = pl.multiple_of((fixed * taken + k) * LANES, LANES)
                parts += [peer[level : level + 1, pl.ds(lane, LANES)] for peer in peers]
            held = jnp.concatenate(parts, axis=0)
            row = jnp.right_shift(jnp.bitwise_xor(owner, device), 5)
            row = row + 4 * jnp.bitwise_and(jnp.right_shift(index, 7), taken - 1)
            column = jnp.bitwise_and(index, LANES - 1)
        angle.append(picked(held, row, column))
    angle = jnp.concatenate(angle, axis=0)
    cos_ref[0:48, :] = jnp.cos(angle)
    sin_ref[0:48, :] = jnp.sin(angle)


def third_angles(x_ref, device):
    rows = [x_ref[pl.ds(third_place(device, h), 1), :] for h in range(8)]
    return jnp.concatenate(rows, axis=0)


def add_rows(x_ref, names, first, count):
    ranks = [first + k for k in range(count)]
    value = jnp.concatenate([x_ref[pl.ds(r, LANES, stride=SLOTS), :] for r in ranks], axis=0)
    name = jnp.concatenate([names[pl.ds(r, 1), :] for r in ranks], axis=1)
    targets = iota((8 * LANES, count * LANES), 0).astype(jnp.float32)
    pick = jnp.where(targets == name, 1.0, 0.0).astype(jnp.bfloat16)
    both = jnp.concatenate(split(value), axis=1)
    return jnp.dot(pick, both, preferred_element_type=jnp.float32)


def chunk_pairs(mask):
    lows = [2 * n - (n & (mask - 1)) for n in range(4)]
    return [(low, low + mask) for low in lows]


def nibble(table, n):
    return (table >> (4 * n)) & 15


def exchange(state, mask, weight):
    lane_set = jnp.bitwise_and(iota((LANES, LANES), 1), weight) != 0
    out = list(state)
    for low, high in chunk_pairs(mask):
        lower, upper = state[low], state[high]
        out[low] = jnp.where(lane_set, pltpu.roll(upper, weight, 1), lower)
        out[high] = jnp.where(lane_set, upper, pltpu.roll(lower, LANES - weight, 1))
    return out


def butterfly(state, mask, high, low, cos_ref, sin_ref, number):
    half = LANES // 2
    stacked = jnp.concatenate(
        [jnp.concatenate([state[pair[c]] for pair in chunk_pairs(mask)], axis=1) for c in range(2)],
        axis=0,
    )
    mixed = product(high, low, stacked)
    out = list(state)
    for n, pair in enumerate(chunk_pairs(mask)):
        for e in range(2):
            block = mixed[e * LANES : (e + 1) * LANES, n * LANES : (n + 1) * LANES]
            real, imag = block[:half], block[half:]
            place = number * 8 + pair[e]
            cosine = cos_ref[place : place + 1, :]
            sine = sin_ref[place : place + 1, :]
            out[pair[e]] = jnp.concatenate(
                [real * cosine - imag * sine, real * sine + imag * cosine], axis=0
            )
    return out


def finish_kernel(
    dev_ref, x_ref, peer0, peer1, peer2, peer3,
    cos_in, sin_in, mats_h_in, mats_l_in,
    out_ref, flag_ref, cos_ref, sin_ref,
    sums, names, cos_far, sin_far, mats_h, mats_l, sems,
):
    pairs = (
        (cos_in, cos_far), (sin_in, sin_far),
        (mats_h_in, mats_h), (mats_l_in, mats_l),
    )
    copies = [pltpu.make_async_copy(a, b, sems.at[n]) for n, (a, b) in enumerate(pairs)]
    for copy in copies:
        copy.start()
    labels = x_ref[pl.ds(LABEL_ROW, LANES, stride=SLOTS), :]
    names[...] = labels.T - 1.0
    flag_ref[0] = jnp.max(names[FLAG_LANE : FLAG_LANE + 1, :] + 1.0).astype(jnp.int32)
    column = iota((LANES, LANES), 1)
    filled = jnp.logical_and(labels > 0.0, column < KEPT)
    most = jnp.max(jnp.where(filled, column + 1, 0).astype(jnp.float32)).astype(jnp.int32)
    sums[...] = add_rows(x_ref, names, 0, SURE)
    angles = x_ref[pl.ds(ANGLE_ROW, LANES, stride=SLOTS), :]
    third = third_angles(x_ref, dev_ref[0])
    peers = (peer0, peer1, peer2, peer3)
    moved_rotations(angles, third, peers, dev_ref[0], cos_ref, sin_ref)
    for first in range(SURE, SLOTS, STEP):

        @pl.when(most > first)
        def _():
            sums[...] += add_rows(x_ref, names, first, STEP)

    for copy in copies:
        copy.wait()
    cos_ref[48:, :] = cos_far[48:, :]
    sin_ref[48:, :] = sin_far[48:, :]
    state = []
    for c in range(8):
        block = sums[c * LANES : (c + 1) * LANES, :]
        state.append((block[:, :LANES] + block[:, LANES:]).T)
    done = 0
    for number in range(7):
        mask = nibble(MASKS, number)
        state = butterfly(state, mask, mats_h[number], mats_l[number], cos_ref, sin_ref, number)
        if number in (2, 5, 6):
            then = nibble(EXCHANGES_TO, number // 3)
            for n in range(done, then):
                state = exchange(state, nibble(MASKS, n), LANES // 2 >> n)
            done = then
    for c in range(8):
        out_ref[c * LANES : (c + 1) * LANES, :] = state[c].T


def finish(arrived, peers, prepared, box_count):
    width = arrived.shape[1]
    table = jax.ShapeDtypeStruct(prepared[0].shape, jnp.float32)
    return pl.pallas_call(
        finish_kernel,
        out_shape=[
            jax.ShapeDtypeStruct((box_count, width), jnp.float32),
            jax.ShapeDtypeStruct((1,), jnp.int32),
            table,
            table,
        ],
        in_specs=in_smem() + in_vmem(5) + anywhere(4),
        out_specs=in_vmem(1) + in_smem() + in_vmem(2),
        scratch_shapes=[
            pltpu.VMEM((box_count, 2 * width), jnp.float32),
            pltpu.VMEM((LANES, LANES), jnp.float32),
        ]
        + [pltpu.VMEM(array.shape, array.dtype) for array in prepared]
        + [pltpu.SemaphoreType.DMA((len(prepared),))],
        compiler_params=params(),
    )(own_number(), arrived, *peers, *prepared)


def collect_kernel(x_ref, before_ref, sums, flag_ref, names):
    labels = x_ref[pl.ds(LABEL_ROW, LANES, stride=SLOTS), :]
    names[...] = labels.T - 1.0
    flag_ref[0] = jnp.max(names[FLAG_LANE : FLAG_LANE + 1, :] + 1.0).astype(jnp.int32)
    names[FLAG_LANE : FLAG_LANE + 1, :] = jnp.full((1, LANES), -1.0)
    sums[...] = before_ref[...]

    def body(pair, carry):
        sums[...] += add_rows(x_ref, names, 2 * pair, 2)
        return carry

    lax.fori_loop(0, SLOTS // 2, body, 0)


def collect(arrived, sums):
    return pl.pallas_call(
        collect_kernel,
        out_shape=[
            jax.ShapeDtypeStruct(sums.shape, jnp.float32),
            jax.ShapeDtypeStruct((1,), jnp.int32),
        ],
        in_specs=in_vmem(2),
        out_specs=in_vmem(1) + in_smem(),
        scratch_shapes=[pltpu.VMEM((LANES, LANES), jnp.float32)],
        compiler_params=params(),
    )(arrived, sums)


def levels_kernel(sums, cos_ref, sin_ref, mats_h, mats_l, out_ref, state):
    half = LANES // 2

    def turn(c, carry):
        block = sums[pl.ds(pl.multiple_of(c * LANES, LANES), LANES), :]
        state[c] = (block[:, :LANES] + block[:, LANES:]).T
        return carry

    lax.fori_loop(0, 8, turn, 0)

    def level(number, carry):
        pairs = chunk_pairs(nibble(MASKS, number))
        stacked = jnp.concatenate(
            [jnp.concatenate([state[pair[c]] for pair in pairs], axis=1) for c in range(2)], axis=0
        )
        mixed = product(mats_h[number], mats_l[number], stacked)
        for n, pair in enumerate(pairs):
            for e in range(2):
                block = mixed[e * LANES : (e + 1) * LANES, n * LANES : (n + 1) * LANES]
                real, imag = block[:half], block[half:]
                cosine = cos_ref[pl.ds(number * 8 + pair[e], 1), :]
                sine = sin_ref[pl.ds(number * 8 + pair[e], 1), :]
                state[pair[e], :half, :] = real * cosine - imag * sine
                state[pair[e], half:, :] = real * sine + imag * cosine
        return carry

    def swap(number, carry):
        weight = half >> number
        lane_set = jnp.bitwise_and(iota((LANES, LANES), 1), weight) != 0
        for low, high in chunk_pairs(nibble(MASKS, number)):
            lower, upper = state[low], state[high]
            state[low] = jnp.where(lane_set, pltpu.roll(upper, weight, 1), lower)
            state[high] = jnp.where(lane_set, upper, pltpu.roll(lower, LANES - weight, 1))
        return carry

    def phase(number, done):
        lax.fori_loop(3 * number, jnp.minimum(3 * number + 3, 7), level, 0)
        then = nibble(EXCHANGES_TO, number)
        lax.fori_loop(done, then, swap, 0)
        return then

    lax.fori_loop(0, 3, phase, 0)

    def write(c, carry):
        out_ref[pl.ds(pl.multiple_of(c * LANES, LANES), LANES), :] = state[c].T
        return carry

    lax.fori_loop(0, 8, write, 0)


def transform(sums, prepared):
    box_count, width = sums.shape[0], sums.shape[1] // 2
    return pl.pallas_call(
        levels_kernel,
        out_shape=jax.ShapeDtypeStruct((box_count, width), jnp.float32),
        in_specs=in_vmem(5),
        out_specs=in_vmem(1)[0],
        scratch_shapes=[pltpu.VMEM((8, width, LANES), jnp.float32)],
        compiler_params=params(),
    )(sums, *prepared)


def in_rounds(sources, owner, box, twiddle, prepared):
    box_count, width = twiddle.shape[1], sources.shape[1]

    def body(carry):
        number, sums, _ = carry
        arrived = deliver(pack(number, sources, owner, box, twiddle))
        return (number + 1, *collect(arrived, sums))

    start = (
        jnp.int32(0),
        jnp.zeros((box_count, 2 * width), jnp.float32),
        jnp.ones((1,), jnp.int32),
    )
    _, sums, _ = lax.while_loop(lambda carry: carry[2][0] > 0, body, start)
    return transform(sums, prepared)


def local(sources, owner, box, leaf_op, level_ops, twiddle):
    box_count = twiddle.shape[1]
    packed = pack(jnp.int32(0), sources, owner, box, twiddle)
    arrived = deliver(packed)
    peers = [twiddle] + [swapped(twiddle, "gx", 4 * i) for i in range(1, 4)]
    prepared = prepare(twiddle, leaf_op, level_ops)
    blocks, flag, *tables = finish(arrived, peers, prepared, box_count)
    return lax.cond(
        flag[0] > 0,
        lambda: in_rounds(sources, owner, box, twiddle, [*tables, *prepared[2:]]),
        lambda: blocks,
    )


def solution(mesh):
    in_specs = (
        P(("gx", "gy"), None),
        P(("gx", "gy"), None),
        P(("gx", "gy")),
        P(),
        P(),
        P(None, ("gx", "gy")),
    )
    out_specs = P(("gx", "gy"), None)
    return jax.shard_map(local, mesh=mesh, in_specs=in_specs, out_specs=out_specs, check_vma=False)
```
